256 devices in a mesh: branch: 2 (over core), seq: 64 (over x_hi, y, z), blk: 2 (over x_lo).
Axes of the slice: x: 4 (x_hi: 2, x_lo: 2; x = x_hi * 2 + x_lo), y: 4, z: 8, core: 2. Of those that a mesh axis runs over, the one named last changes fastest.
Arguments:
- query: bfloat16 [2, 4608, 3072], P('branch', ('seq', 'blk')), may hold values from -10 to 10
- key: bfloat16 [2, 4608, 3072], P('branch', ('seq', 'blk')), may hold values from -10 to 10
- value: bfloat16 [2, 4608, 3072], P('branch', ('seq', 'blk')), may hold values from -6 to 6
- out_weight: bfloat16 [3072, 3072], P('blk'), may hold values from -0.109375 to 0.109375
Outputs:
- guided: bfloat16 [4608, 3072], P(('seq', 'blk'), 'branch')
The draws below stay inside these ranges and needn't reach their ends.
All inputs are finite; a program needn't handle non-finite values.
Results may differ from the reference program's by a relative error of at most 0.015.
Values may be sent and summed in bfloat16 or wider, within the bound.
A program may use at most 256 MiB of HBM per device.

```python
import jax
import jax.numpy as jnp
from jax import lax

HEADS = 24
HD = 128
D = 3072
GRIDW = 256
TOKENS = 4608


def draw_key(key, part):
    key = jax.random.fold_in(key, 3)
    base = jnp.clip(1.5 * jax.random.normal(key, (2, TOKENS, HEADS * HD), jnp.float32), -6.0, 6.0)
    return base.astype(jnp.bfloat16)


def draw_query(key, part):
    key = jax.random.fold_in(key, 5)
    base = jnp.clip(1.5 * jax.random.normal(key, (2, TOKENS, HEADS * HD), jnp.float32), -6.0, 6.0)
    return base.astype(jnp.bfloat16)


def block_scale(key, extent, shards, low, largest):
    def one(axis_at, shards_of):
        heights = jax.random.uniform(jax.random.fold_in(jax.random.fold_in(key, 6), axis_at), (shards_of,), jnp.float32, low / len(shards), largest / len(shards))
        return jnp.repeat(jnp.exp(heights), extent[axis_at] // shards_of).reshape((-1,) + (1,) * (len(extent) - axis_at - 1))

    loudness = one(*shards[0])
    for cut in shards[1:]:
        loudness = loudness * one(*cut)
    return loudness


def noise(rng, shape, width, most, cuts=(), kind=jnp.bfloat16):
    drawn = jax.random.normal(rng, shape, jnp.float32) * width
    if len(cuts) > 0:
        drawn = block_scale(rng, shape, cuts, -0.22, 0.18) * drawn
    return jnp.clip(drawn, min=-most, max=most).astype(kind)


def setup_inputs(seed: int = 0) -> dict:
    key_of = jax.random.split(jax.random.key(seed), 5)
    return {
        "query": draw_query(jax.random.fold_in(key_of[4], 71), 0),
        "key": draw_key(jax.random.fold_in(key_of[4], 71), 0),
        "value": noise(key_of[2], (2, TOKENS, D), 1.0, 6.0, ((0, 2), (1, 128))),
        "out_weight": noise(key_of[3], (D, D), D ** -0.5, 0.109375, ((0, 2),)),
    }


guidance = 4.0


def pair_angles(positions):
    time_dim = HD // 8
    side_dim = (HD - time_dim) // 2
    index = jnp.arange(side_dim // 2).astype(jnp.float32)
    freq = jnp.power(jnp.float32(10000.0), -2.0 * index / side_dim).astype(jnp.float32)
    row_at = (positions // GRIDW).astype(jnp.float32)
    col_at = (positions % GRIDW).astype(jnp.float32)
    still = jnp.zeros((positions.shape[0], time_dim // 2), jnp.float32)
    return jnp.concatenate([still, row_at[:, None] * freq[None, :], col_at[:, None] * freq[None, :]], axis=1)


def rotate(values, positions):
    count = values.shape[0]
    pairs = values.astype(jnp.float32).reshape(count, -1, HD // 2, 2)
    angle = pair_angles(positions)[:, None, :]
    cosine = jnp.cos(angle)
    sine = jnp.sin(angle)
    first = pairs[..., 0] * cosine - pairs[..., 1] * sine
    second = pairs[..., 0] * sine + pairs[..., 1] * cosine
    return jnp.stack([first, second], axis=-1).reshape(count, -1).astype(jnp.bfloat16)


def head_attention(triple):
    q_head, k_head, v_head = triple
    scores = jnp.dot(q_head, k_head.T, preferred_element_type=jnp.float32) * (HD ** -0.5)
    top = jnp.max(scores, axis=1, keepdims=True)
    expo = jnp.exp(scores - top)
    total = jnp.sum(expo, axis=1, keepdims=True)
    mixed = jnp.dot(expo.astype(jnp.bfloat16), v_head, preferred_element_type=jnp.float32) / total
    return mixed.astype(jnp.bfloat16)


def rounded(term):
    return lax.optimization_barrier(term.astype(jnp.bfloat16)).astype(jnp.float32)


def one_branch(query, key, value, out_weight):
    positions = jnp.arange(TOKENS, dtype=jnp.int32)
    turned_q = rotate(query, positions).reshape(TOKENS, HEADS, HD).transpose(1, 0, 2)
    turned_k = rotate(key, positions).reshape(TOKENS, HEADS, HD).transpose(1, 0, 2)
    v_heads = value.reshape(TOKENS, HEADS, HD).transpose(1, 0, 2)
    attended = lax.map(head_attention, (turned_q, turned_k, v_heads))
    attended = attended.transpose(1, 0, 2).reshape(TOKENS, HEADS * HD)
    half = HEADS * HD // 2
    low_part = rounded(jnp.dot(attended[:, :half], out_weight[:half], preferred_element_type=jnp.float32))
    high_part = rounded(jnp.dot(attended[:, half:], out_weight[half:], preferred_element_type=jnp.float32))
    return (low_part + high_part).astype(jnp.bfloat16)


def reference(query, key, value, out_weight):
    cond = one_branch(query[0], key[0], value[0], out_weight).astype(jnp.float32)
    uncond = one_branch(query[1], key[1], value[1], out_weight).astype(jnp.float32)
    return (uncond + guidance * (cond - uncond)).astype(jnp.bfloat16)
```

```python
import functools

import jax
import jax.numpy as jnp
import numpy as np
from jax import lax
from jax.experimental import pallas as pl
from jax.experimental.pallas import tpu as pltpu
from jax.sharding import PartitionSpec as P

HD = 128
GRIDW = 256
GUIDANCE = 4.0
F32 = jnp.float32
BF16 = jnp.bfloat16
MESH = pl.DeviceIdType.MESH

NJ = 3
NZ = 8
NY = 4
ROWS = 36
MAIN = 32
REM = ROWS - MAIN
TOK = NZ * ROWS
QS = 4 * TOK
KS = NY * TOK
QT = 384
WIN = 384
SCALE = float(HD**-0.5 / np.log(2.0))


def tables(places):
    time_dim = HD // 8
    side_dim = (HD - time_dim) // 2
    index = np.arange(side_dim // 2).astype(np.float32)
    freq = np.power(np.float32(10000.0), -2.0 * index / side_dim).astype(np.float32)
    at = np.arange(places * ROWS)
    row = (at // GRIDW).astype(np.float32)[:, None] * freq[None, :]
    col = (at % GRIDW).astype(np.float32)[:, None] * freq[None, :]
    still = np.zeros((places * ROWS, time_dim // 2), np.float32)
    angle = np.repeat(np.concatenate([still, row, col], axis=1), 2, axis=1).astype(np.float64)
    sign = np.where(np.arange(HD) % 2 == 0, -1.0, 1.0)
    both = np.stack([np.cos(angle), np.sin(angle) * sign]).astype(np.float32)
    out = np.zeros((places, 2, 40, HD), np.float32)
    out[:, :, :ROWS] = both.reshape(2, places, ROWS, HD).transpose(1, 0, 2, 3)
    return out


def turn(x, cos, sin):
    even = lax.broadcasted_iota(jnp.int32, x.shape, 1) % 2 == 0
    swapped = jnp.where(even, pltpu.roll(x, HD - 1, 1), pltpu.roll(x, 1, 1))
    return x * cos + swapped * sin


def pick(shape, source):
    row = lax.broadcasted_iota(jnp.int32, shape, 0)
    col = lax.broadcasted_iota(jnp.int32, shape, 1)
    return jnp.where(col == source(row), 1.0, 0.0).astype(BF16)


def dot(a, b):
    return jnp.dot(a, b, preferred_element_type=F32)


def kernel(
    q_ref, k_ref, v_ref, w_ref, tab_ref, o_ref,
    tab, rtab, send_a, recv_a, qall, kv, vt, obuf, stat, mo, mst, wt, cbuf, recv_c, sib_c, gbuf,
    acc, dsend, drecv, wv,
    tab_sem, w_sem, a_send, a_recv, q_send, q_recv, kv_send, kv_recv, f_send, f_recv,
    m_send, m_recv, n_send, n_recv, c_send, c_recv, s_send, s_recv, d_send, d_recv,
):
    c = lax.axis_index("branch")
    s = lax.axis_index("seq")
    xl = lax.axis_index("blk")
    xh = s // 32
    y = (s // 8) % 4
    z = s % 8
    place = s * 2 + xl
    slot = c * 2 + xl

    tab_copy = pltpu.make_async_copy(tab_ref.at[place], tab, tab_sem)
    tab_copy.start()
    w_copies = []
    for j in range(NJ):
        for t in range(4):
            w_copies.append(
                pltpu.make_async_copy(
                    w_ref.at[pl.ds((t * NJ + j) * HD, HD), pl.ds(pl.multiple_of(c * 1536, 1536), 1536)],
                    wv.at[j, pl.ds(t * HD, HD)],
                    w_sem.at[j, t],
                )
            )
            w_copies[-1].start()

    def far(zz, blk):
        return (xh, (c * 4 + y) * 8 + zz, blk)

    def ring(step):
        return (c, (xh * 4 + (y + step) % 4) * 8 + z, xl)

    def near(step):
        other = (slot + step) % 4
        return (other // 2, s, other % 2), other

    barrier = pltpu.get_barrier_semaphore()

    @pl.loop(0, NZ)
    def _(zz):
        for blk in range(2):
            @pl.when(jnp.logical_not((xh == c) & (zz == z) & (xl == blk)))
            def _():
                pl.semaphore_signal(barrier, inc=1, device_id=far(zz, blk), device_id_type=MESH)

    for step in range(1, 4):
        pl.semaphore_signal(barrier, inc=1, device_id=ring(step), device_id_type=MESH)
        pl.semaphore_signal(barrier, inc=1, device_id=near(step)[0], device_id_type=MESH)

    def own(zz):
        return (xh == c) & (zz == z)

    def a_copy(j, zz):
        return pltpu.make_async_remote_copy(
            src_ref=send_a.at[j, zz], dst_ref=recv_a.at[j, z],
            send_sem=a_send.at[j, zz], recv_sem=a_recv.at[j, z],
            device_id=far(zz, xl), device_id_type=MESH,
        )

    def a_local(j):
        return pltpu.make_async_copy(send_a.at[j, z], recv_a.at[j, z], a_recv.at[j, z])

    def a_arrival(j, zz):
        return pltpu.make_async_remote_copy(
            src_ref=send_a.at[j, zz], dst_ref=recv_a.at[j, zz],
            send_sem=a_send.at[j, zz], recv_sem=a_recv.at[j, zz],
            device_id=far(zz, xl), device_id_type=MESH,
        )

    tab_copy.wait()
    rtab[0, 0:4] = tab[0, 32:36] * SCALE
    rtab[0, 4:8] = tab[0, 32:36]
    rtab[1, 0:4] = tab[1, 32:36] * SCALE
    rtab[1, 4:8] = tab[1, 32:36]

    def prepare(j):
        @pl.loop(0, NZ)
        def _(zz):
            cols = pl.ds(pl.multiple_of((zz * NJ + j) * HD, HD), HD)
            cos, sin = tab[0, 0:MAIN], tab[1, 0:MAIN]
            q = turn(q_ref[0, 0:MAIN, cols].astype(F32), cos * SCALE, sin * SCALE)
            k = turn(k_ref[0, 0:MAIN, cols].astype(F32), cos, sin)
            send_a[j, zz, 0:32] = q.astype(BF16)
            send_a[j, zz, 32:64] = k.astype(BF16)
            send_a[j, zz, 64:96] = v_ref[0, 0:MAIN, cols]
            qk = jnp.concatenate(
                [q_ref[0, MAIN:ROWS, cols].astype(F32), k_ref[0, MAIN:ROWS, cols].astype(F32)], axis=0
            )
            v4 = v_ref[0, MAIN:ROWS, cols].astype(F32)
            rest = jnp.concatenate([turn(qk, rtab[0], rtab[1]), v4, jnp.zeros_like(v4)], axis=0)
            send_a[j, zz, 96:112] = rest.astype(BF16)

    def depart(j):
        @pl.loop(1, NZ + 1)
        def _(i):
            zz = (z + i) % NZ

            @pl.when(own(zz))
            def _():
                a_local(j).start()

            @pl.when(jnp.logical_not(own(zz)))
            def _():
                a_copy(j, zz).start()

    prepare(0)
    pl.semaphore_wait(barrier, jnp.where(xh == c, 21, 22))
    depart(0)
    for j in range(1, NJ):
        prepare(j)
        depart(j)

    def q_copy(j, step):
        device, other = near(step)
        return pltpu.make_async_remote_copy(
            src_ref=qall.at[j, slot], dst_ref=qall.at[j, slot],
            send_sem=q_send.at[j, step - 1], recv_sem=q_recv.at[j, 3 - step],
            device_id=device, device_id_type=MESH,
        )

    def q_arrival(j, step):
        device, other = near(step)
        return pltpu.make_async_remote_copy(
            src_ref=qall.at[j, slot], dst_ref=qall.at[j, other],
            send_sem=q_send.at[j, step - 1], recv_sem=q_recv.at[j, step - 1],
            device_id=device, device_id_type=MESH,
        )

    def kv_copy(j, way):
        return pltpu.make_async_remote_copy(
            src_ref=kv.at[j, 0], dst_ref=kv.at[j, 1 + way],
            send_sem=kv_send.at[j, way], recv_sem=kv_recv.at[j, way],
            device_id=ring(1 if way == 0 else 3), device_id_type=MESH,
        )

    def f_copy(j, way):
        return pltpu.make_async_remote_copy(
            src_ref=kv.at[j, 1 + way, way], dst_ref=kv.at[j, 3, way],
            send_sem=f_send.at[j, way], recv_sem=f_recv.at[j, way],
            device_id=ring(1 if way == 0 else 3), device_id_type=MESH,
        )

    def gather(j):
        for zz in range(NZ):
            a_arrival(j, zz).wait_recv()
        for zz in range(NZ):
            kv[j, 0, 0, zz * 32 : zz * 32 + 32] = recv_a[j, zz, 32:64]
            kv[j, 0, 1, zz * 32 : zz * 32 + 32] = recv_a[j, zz, 64:96]
            qall[j, slot, zz * 32 : zz * 32 + 32] = recv_a[j, zz, 0:32]
        rest = recv_a[j, :, 96:112, :].reshape(NZ * 16, HD)
        order = pick((96, 128), lambda r: (r % 32) // 4 * 16 + r // 32 * 4 + r % 4)
        rest = dot(order, rest).astype(BF16)
        kv[j, 0, 0, 256:288] = rest[32:64]
        kv[j, 0, 1, 256:288] = rest[64:96]
        qall[j, slot, 256:288] = rest[0:32]
        for way in range(2):
            kv_copy(j, way).start()
        for step in range(1, 4):
            q_copy(j, step).start()

    def forward(j):
        for way in range(2):
            kv_copy(j, way).wait_recv()
            f_copy(j, way).start()

    def m_copies(j, step):
        device, other = near(step)
        return (
            pltpu.make_async_remote_copy(
                src_ref=obuf.at[j, pl.ds(pl.multiple_of(other * TOK, 32), TOK)], dst_ref=mo.at[j, slot],
                send_sem=m_send.at[j, step - 1], recv_sem=m_recv.at[j, 3 - step],
                device_id=device, device_id_type=MESH,
            ),
            pltpu.make_async_remote_copy(
                src_ref=stat.at[j, :, pl.ds(pl.multiple_of(other * 256, 256), WIN)], dst_ref=mst.at[j, slot],
                send_sem=n_send.at[j, step - 1], recv_sem=n_recv.at[j, 3 - step],
                device_id=device, device_id_type=MESH,
            ),
        )

    def m_arrivals(j, step):
        device, other = near(step)
        return (
            pltpu.make_async_remote_copy(
                src_ref=mo.at[j, slot], dst_ref=mo.at[j, other],
                send_sem=m_send.at[j, step - 1], recv_sem=m_recv.at[j, step - 1],
                device_id=device, device_id_type=MESH,
            ),
            pltpu.make_async_remote_copy(
                src_ref=mst.at[j, slot], dst_ref=mst.at[j, other],
                send_sem=n_send.at[j, step - 1], recv_sem=n_recv.at[j, step - 1],
                device_id=device, device_id_type=MESH,
            ),
        )

    def attend(j):
        for step in range(1, 4):
            q_arrival(j, step).wait_recv()
        for way in range(2):
            f_copy(j, way).wait_recv()
        for t in range(NY):
            vt[:, t * TOK : (t + 1) * TOK] = kv[j, t, 1].astype(F32).T.astype(BF16)
        stat[j] = jnp.zeros((8, QS), F32)
        queries = qall.at[j].reshape(QS, HD)

        @pl.loop(0, QS // QT)
        def _(t):
            rows = pl.ds(pl.multiple_of(t * QT, QT), QT)
            q = queries[rows, :]
            keys = kv[j, :, 0].reshape(KS, HD)
            scores = lax.dot_general(keys, q, (((1,), (1,)), ((), ())), preferred_element_type=F32)
            top = jnp.max(scores, axis=0, keepdims=True)
            expo = jnp.exp2(scores - top)
            total = jnp.sum(expo, axis=0, keepdims=True)
            mixed = dot(vt[...], expo.astype(BF16)) / total
            stat[j, 0:1, rows] = top
            stat[j, 1:2, rows] = total
            obuf[j, rows, :] = mixed.T.astype(BF16)

        for step in range(1, 4):
            for copy in m_copies(j, step):
                copy.start()
        mo[j, slot] = obuf[j, pl.ds(pl.multiple_of(slot * TOK, 32), TOK), :]
        mst[j, slot] = stat[j, :, pl.ds(pl.multiple_of(slot * 256, 256), WIN)]

    def c_copy(j, zz):
        return pltpu.make_async_remote_copy(
            src_ref=cbuf.at[j, zz], dst_ref=recv_c.at[j, xl, z % 4],
            send_sem=c_send.at[j, zz], recv_sem=c_recv.at[j, xl, z % 4],
            device_id=far(zz, z // 4), device_id_type=MESH,
        )

    def c_own(zz):
        return (xh == c) & (zz == z) & (z // 4 == xl)

    def merge(j):
        for step in range(1, 4):
            for copy in m_arrivals(j, step):
                copy.wait_recv()
        tops = [mst[j, i, 0:1, :] for i in range(4)]
        top = jnp.maximum(jnp.maximum(tops[0], tops[1]), jnp.maximum(tops[2], tops[3]))
        parts = [mst[j, i, 1:2, :] * jnp.exp2(tops[i] - top) for i in range(4)]
        total = (parts[0] + parts[1]) + (parts[2] + parts[3])
        share = jnp.concatenate([p / total for p in parts] + [jnp.zeros((124, WIN), F32)], axis=0)
        wt[...] = share.T
        share = wt[pl.ds(pl.multiple_of(slot * 32, 32), TOK), :]
        mixed = share[:, 0:1] * mo[j, 0].astype(F32)
        for i in range(1, 4):
            mixed += share[:, i : i + 1] * mo[j, i].astype(F32)
        mixed = mixed.astype(BF16)
        order = pick((128, 32), lambda r: jnp.where(r % 16 < 4, r // 16 * 4 + r % 16, -1))
        rest = dot(order, mixed[256:288]).astype(BF16)
        for zz in range(NZ):
            cbuf[j, zz, 0:32] = mixed[zz * 32 : zz * 32 + 32]
            cbuf[j, zz, 32:48] = rest[zz * 16 : zz * 16 + 16]

        @pl.loop(1, NZ + 1)
        def _(i):
            zz = (z + i) % NZ

            @pl.when(c_own(zz))
            def _():
                pltpu.make_async_copy(cbuf.at[j, z], recv_c.at[j, xl, z % 4], c_recv.at[j, xl, z % 4]).start()

            @pl.when(jnp.logical_not(c_own(zz)))
            def _():
                c_copy(j, zz).start()

    sibling = (1 - c, s, xl)

    def s_copy(j):
        return pltpu.make_async_remote_copy(
            src_ref=recv_c.at[j], dst_ref=sib_c.at[j],
            send_sem=s_send.at[j], recv_sem=s_recv.at[j],
            device_id=sibling, device_id_type=MESH,
        )

    def share_out(j):
        for blk in range(2):
            for t in range(4):
                pltpu.make_async_remote_copy(
                    src_ref=cbuf.at[j, 0], dst_ref=recv_c.at[j, blk, t],
                    send_sem=c_send.at[j, 0], recv_sem=c_recv.at[j, blk, t],
                    device_id=sibling, device_id_type=MESH,
                ).wait_recv()
        s_copy(j).start()

    mine = jnp.where(c == 0, GUIDANCE, 1.0 - GUIDANCE)
    theirs = 1.0 - mine

    def guide(j):
        s_copy(j).wait_recv()
        for blk in range(2):
            for t in range(4):
                g = mine * recv_c[j, blk, t].astype(F32) + theirs * sib_c[j, blk, t].astype(F32)
                gbuf[blk * 48 : blk * 48 + 48, t * HD : (t + 1) * HD] = g.astype(BF16)
        for t in range(4):
            w_copies[j * 4 + t].wait()

    def d_copy(n):
        return pltpu.make_async_remote_copy(
            src_ref=dsend.at[n], dst_ref=drecv.at[n],
            send_sem=d_send.at[n], recv_sem=d_recv.at[n],
            device_id=(c, s, 1 - xl), device_id_type=MESH,
        )

    def project(j):
        guide(j)
        for n in range(3):
            part = dot(gbuf[...], wv[j, :, n * 512 : (n + 1) * 512])
            if j > 0:
                part += acc[n]
            acc[n] = part
            if j == NJ - 1:
                dsend[n] = acc[n, pl.ds(pl.multiple_of((1 - xl) * 48, 16), 48), :].astype(BF16)
                d_copy(n).start()

    gather(0)
    forward(0)
    gather(1)
    attend(0)
    forward(1)
    gather(2)
    attend(1)
    forward(2)
    merge(0)
    attend(2)
    merge(1)
    share_out(0)
    project(0)
    merge(2)
    share_out(1)
    project(1)
    share_out(2)
    project(2)

    for n in range(3):
        d_copy(n).wait_recv()
        full = acc[n, pl.ds(pl.multiple_of(xl * 48, 16), 48), :] + drecv[n].astype(F32)
        o_ref[:, n * 512 : (n + 1) * 512] = full[0:ROWS].astype(BF16)

    for j in range(NJ):
        @pl.loop(0, NZ)
        def _(zz):
            @pl.when(jnp.logical_not(own(zz)))
            def _():
                a_copy(j, zz).wait_send()

            @pl.when(jnp.logical_not(c_own(zz)))
            def _():
                c_copy(j, zz).wait_send()

        for step in range(1, 4):
            q_copy(j, step).wait_send()
            for copy in m_copies(j, step):
                copy.wait_send()
        for way in range(2):
            kv_copy(j, way).wait_send()
            f_copy(j, way).wait_send()
        s_copy(j).wait_send()
    for n in range(3):
        d_copy(n).wait_send()


def shards(query, key, value, out_weight, table):
    vmem = pl.BlockSpec(memory_space=pltpu.VMEM)
    hbm = pl.BlockSpec(memory_space=pl.ANY)
    dma = pltpu.SemaphoreType.DMA
    return pl.pallas_call(
        kernel,
        out_shape=jax.ShapeDtypeStruct((ROWS, 1536), BF16),
        in_specs=[vmem, vmem, vmem, hbm, hbm],
        out_specs=vmem,
        scratch_shapes=[
            pltpu.VMEM((2, 40, HD), F32),
            pltpu.VMEM((2, 8, HD), F32),
            pltpu.VMEM((NJ, NZ, 112, HD), BF16),
            pltpu.VMEM((NJ, NZ, 112, HD), BF16),
            pltpu.VMEM((NJ, 4, TOK, HD), BF16),
            pltpu.VMEM((NJ, NY, 2, TOK, HD), BF16),
            pltpu.VMEM((HD, KS), BF16),
            pltpu.VMEM((NJ, QS, HD), BF16),
            pltpu.VMEM((NJ, 8, QS), F32),
            pltpu.VMEM((NJ, 4, TOK, HD), BF16),
            pltpu.VMEM((NJ, 4, 8, WIN), F32),
            pltpu.VMEM((WIN, HD), F32),
            pltpu.VMEM((NJ, NZ, 48, HD), BF16),
            pltpu.VMEM((NJ, 2, 4, 48, HD), BF16),
            pltpu.VMEM((NJ, 2, 4, 48, HD), BF16),
            pltpu.VMEM((96, 512), BF16),
            pltpu.VMEM((3, 96, 512), F32),
            pltpu.VMEM((3, 48, 512), BF16),
            pltpu.VMEM((3, 48, 512), BF16),
            pltpu.VMEM((NJ, 512, 1536), BF16),
            dma(()), dma((NJ, 4)),
            dma((NJ, NZ)), dma((NJ, NZ)),
            dma((NJ, 3)), dma((NJ, 3)),
            dma((NJ, 2)), dma((NJ, 2)),
            dma((NJ, 2)), dma((NJ, 2)),
            dma((NJ, 3)), dma((NJ, 3)),
            dma((NJ, 3)), dma((NJ, 3)),
            dma((NJ, NZ)), dma((NJ, 2, 4)),
            dma((NJ,)), dma((NJ,)),
            dma((3,)), dma((3,)),
        ],
        compiler_params=pltpu.CompilerParams(
            collective_id=0, has_side_effects=True, vmem_limit_bytes=48 * 1024 * 1024
        ),
        cost_estimate=pl.CostEstimate(flops=2_400_000_000, bytes_accessed=8_000_000, transcendentals=4_000_000),
    )(query, key, value, out_weight, table)


def solution(mesh):
    places = mesh.shape["seq"] * mesh.shape["blk"]
    call = jax.shard_map(
        shards,
        mesh=mesh,
        in_specs=(
            P("branch", ("seq", "blk"), None),
            P("branch", ("seq", "blk"), None),
            P("branch", ("seq", "blk"), None),
            P("blk", None),
            P(),
        ),
        out_specs=P(("seq", "blk"), "branch"),
        check_vma=False,
    )

    def run(query, key, value, out_weight):
        return call(query, key, value, out_weight, jnp.asarray(tables(places)))

    return run
```

```python
import functools

import jax
import jax.numpy as jnp
import numpy as np
from jax import lax
from jax.experimental import pallas as pl
from jax.experimental.pallas import tpu as pltpu
from jax.sharding import PartitionSpec as P

HD = 128
GRIDW = 256
GUIDANCE = 4.0
F32 = jnp.float32
BF16 = jnp.bfloat16
MESH = pl.DeviceIdType.MESH

NJ = 3
NZ = 8
NY = 4
ROWS = 36
MAIN = 32
REM = ROWS - MAIN
TOK = NZ * ROWS
QS = 4 * TOK
KS = NY * TOK
PART = (0, 48, 80, 112)
SCALE = float(HD**-0.5 / np.log(2.0))


def tables(places):
    time_dim = HD // 8
    side_dim = (HD - time_dim) // 2
    index = np.arange(side_dim // 2).astype(np.float32)
    freq = np.power(np.float32(10000.0), -2.0 * index / side_dim).astype(np.float32)
    at = np.arange(places * ROWS)
    row = (at // GRIDW).astype(np.float32)[:, None] * freq[None, :]
    col = (at % GRIDW).astype(np.float32)[:, None] * freq[None, :]
    still = np.zeros((places * ROWS, time_dim // 2), np.float32)
    angle = np.repeat(np.concatenate([still, row, col], axis=1), 2, axis=1).astype(np.float64)
    sign = np.where(np.arange(HD) % 2 == 0, -1.0, 1.0)
    both = np.stack([np.cos(angle), np.sin(angle) * sign]).astype(np.float32)
    out = np.zeros((places, 2, 40, HD), np.float32)
    out[:, :, :ROWS] = both.reshape(2, places, ROWS, HD).transpose(1, 0, 2, 3)
    return out


def turn(x, cos, sin):
    even = lax.broadcasted_iota(jnp.int32, x.shape, 1) % 2 == 0
    swapped = jnp.where(even, pltpu.roll(x, HD - 1, 1), pltpu.roll(x, 1, 1))
    return x * cos + swapped * sin


def pick(shape, source):
    row = lax.broadcasted_iota(jnp.int32, shape, 0)
    col = lax.broadcasted_iota(jnp.int32, shape, 1)
    return jnp.where(col == source(row), 1.0, 0.0).astype(BF16)


def outward(i):
    return jnp.where(i % 2 == 1, 4 - (i + 1) // 2, 4 + i // 2)


def dot(a, b):
    return jnp.dot(a, b, preferred_element_type=F32)


def kernel(
    q_hbm, k_hbm, v_hbm, w_ref, tab_ref, o_ref,
    q_ref, k_ref, v_ref, tab, rtab, send_a, recv_a, qall, kv, vt, obuf, pst, mo, mst, wt, cbuf,
    recv_c, sib_c, gbuf, acc, dsend, drecv, dsend4, drecv4, wv,
    in_sem, w_sem, a_send, a_recv, q_send, q_recv, y_send, y_recv, f_send, f_recv,
    m_send, m_recv, n_send, n_recv, c_send, c_recv, s_send, s_recv, d_send, d_recv,
):
    c = lax.axis_index("branch")
    s = lax.axis_index("seq")
    xl = lax.axis_index("blk")
    xh = s // 32
    y = (s // 8) % 4
    z = s % 8
    place = s * 2 + xl
    slot = xl * 2 + c

    def far(zz, blk):
        return (xh, (c * 4 + y) * 8 + zz, blk)

    def ring(step):
        return (c, (xh * 4 + (y + step) % 4) * 8 + z, xl)

    def near(step):
        device = ((c + step) % 2, s, (xl + step // 2) % 2)
        return device, device[2] * 2 + device[0]

    barrier = pltpu.get_barrier_semaphore()

    @pl.loop(0, NZ)
    def _(zz):
        for blk in range(2):
            @pl.when(jnp.logical_not((xh == c) & (zz == z) & (xl == blk)))
            def _():
                pl.semaphore_signal(barrier, inc=1, device_id=far(zz, blk), device_id_type=MESH)

    for step in range(1, 4):
        pl.semaphore_signal(barrier, inc=1, device_id=ring(step), device_id_type=MESH)
        pl.semaphore_signal(barrier, inc=1, device_id=near(step)[0], device_id_type=MESH)

    loads = [
        pltpu.make_async_copy(src, dst, in_sem.at[i])
        for i, (src, dst) in enumerate(
            ((tab_ref.at[place], tab), (k_hbm.at[0], k_ref), (q_hbm.at[0], q_ref), (v_hbm.at[0], v_ref))
        )
    ]
    for load in loads:
        load.start()
    w_copies = []
    for j in range(NJ):
        for t in range(4):
            w_copies.append(
                pltpu.make_async_copy(
                    w_ref.at[pl.ds((t * NJ + j) * HD, HD), pl.ds(pl.multiple_of(c * 1536, 1536), 1536)],
                    wv.at[j, pl.ds(t * HD, HD)],
                    w_sem.at[j, t],
                )
            )
            w_copies[-1].start()

    def own(zz):
        return (xh == c) & (zz == z)

    def a_copy(j, p, zz):
        rows = pl.ds(PART[p], PART[p + 1] - PART[p])
        return pltpu.make_async_remote_copy(
            src_ref=send_a.at[j, zz, rows], dst_ref=recv_a.at[j, z, rows],
            send_sem=a_send.at[j, p, zz], recv_sem=a_recv.at[j, p, z],
            device_id=far(zz, xl), device_id_type=MESH,
        )

    def a_local(j, p):
        rows = pl.ds(PART[p], PART[p + 1] - PART[p])
        return pltpu.make_async_copy(send_a.at[j, z, rows], recv_a.at[j, z, rows], a_recv.at[j, p, z])

    def a_arrival(j, p, zz):
        rows = pl.ds(PART[p], PART[p + 1] - PART[p])
        return pltpu.make_async_remote_copy(
            src_ref=send_a.at[j, zz, rows], dst_ref=recv_a.at[j, zz, rows],
            send_sem=a_send.at[j, p, zz], recv_sem=a_recv.at[j, p, zz],
            device_id=far(zz, xl), device_id_type=MESH,
        )

    for load in loads:
        load.wait()
    rtab[0, 0:4] = tab[0, 32:36] * SCALE
    rtab[0, 4:8] = tab[0, 32:36]
    rtab[1, 0:4] = tab[1, 32:36] * SCALE
    rtab[1, 4:8] = tab[1, 32:36]

    def prepare(j):
        @pl.loop(0, NZ)
        def _(zz):
            cols = pl.ds(pl.multiple_of((zz * NJ + j) * HD, HD), HD)
            cos, sin = tab[0, 0:MAIN], tab[1, 0:MAIN]
            q = turn(q_ref[0:MAIN, cols].astype(F32), cos * SCALE, sin * SCALE)
            k = turn(k_ref[0:MAIN, cols].astype(F32), cos, sin)
            send_a[j, zz, 0:32] = k.astype(BF16)
            send_a[j, zz, 48:80] = v_ref[0:MAIN, cols]
            send_a[j, zz, 80:112] = q.astype(BF16)
            qk = jnp.concatenate(
                [q_ref[MAIN:ROWS, cols].astype(F32), k_ref[MAIN:ROWS, cols].astype(F32)], axis=0
            )
            v4 = v_ref[MAIN:ROWS, cols].astype(F32)
            rest = jnp.concatenate([turn(qk, rtab[0], rtab[1]), v4, jnp.zeros_like(v4)], axis=0)
            send_a[j, zz, 32:48] = rest.astype(BF16)

    def depart(j, p):
        @pl.loop(0, NZ)
        def _(i):
            zz = (z + outward(i)) % NZ

            @pl.when(own(zz))
            def _():
                a_local(j, p).start()

            @pl.when(jnp.logical_not(own(zz)))
            def _():
                a_copy(j, p, zz).start()

    def y_copy(j, p, way):
        return pltpu.make_async_remote_copy(
            src_ref=kv.at[j, 0, p], dst_ref=kv.at[j, 1 + way, p],
            send_sem=y_send.at[j, p, way], recv_sem=y_recv.at[j, p, way],
            device_id=ring(1 if way == 0 else 3), device_id_type=MESH,
        )

    def f_copy(j, p, way):
        rows = pl.ds(way * 144, 144)
        return pltpu.make_async_remote_copy(
            src_ref=kv.at[j, 1 + way, p, rows], dst_ref=kv.at[j, 3, p, rows],
            send_sem=f_send.at[j, p, way], recv_sem=f_recv.at[j, p, way],
            device_id=ring(1 if way == 0 else 3), device_id_type=MESH,
        )

    def q_copy(j, step):
        which = near(2)[1] if step == 3 else slot
        return pltpu.make_async_remote_copy(
            src_ref=qall.at[j, which], dst_ref=qall.at[j, which],
            send_sem=q_send.at[j, step - 1], recv_sem=q_recv.at[j, step - 1],
            device_id=near(2 if step == 2 else 1)[0], device_id_type=MESH,
        )

    def gather(j, p):
        for zz in range(NZ):
            a_arrival(j, p, zz).wait_recv()
        if p == 0:
            for zz in range(NZ):
                kv[j, 0, 0, zz * 32 : zz * 32 + 32] = recv_a[j, zz, 0:32]
            rest = recv_a[j, :, 32:48, :].reshape(NZ * 16, HD)
            order = pick((96, 128), lambda r: (r % 32) // 4 * 16 + r // 32 * 4 + r % 4)
            rest = dot(order, rest).astype(BF16)
            kv[j, 0, 0, 256:288] = rest[32:64]
            kv[j, 0, 1, 256:288] = rest[64:96]
            qall[j, slot, 256:288] = rest[0:32]
        elif p == 1:
            for zz in range(NZ):
                kv[j, 0, 1, zz * 32 : zz * 32 + 32] = recv_a[j, zz, 48:80]
        else:
            for zz in range(NZ):
                qall[j, slot, zz * 32 : zz * 32 + 32] = recv_a[j, zz, 80:112]
        if p < 2:
            for way in range(2):
                y_copy(j, p, way).start()
        else:
            for step in (2, 1):
                q_copy(j, step).start()

    def forward(j, p):
        if p < 2:
            for way in range(2):
                y_copy(j, p, way).wait_recv()
                f_copy(j, p, way).start()
        else:
            q_copy(j, 2).wait_recv()
            q_copy(j, 3).start()

    def m_copies(j, step):
        device, other = near(step)
        return (
            pltpu.make_async_remote_copy(
                src_ref=obuf.at[j, pl.ds(pl.multiple_of(other * TOK, 32), TOK)], dst_ref=mo.at[j, slot],
                send_sem=m_send.at[j, step - 1], recv_sem=m_recv.at[j, step - 1],
                device_id=device, device_id_type=MESH,
            ),
            pltpu.make_async_remote_copy(
                src_ref=pst.at[j, other], dst_ref=mst.at[j, slot],
                send_sem=n_send.at[j, step - 1], recv_sem=n_recv.at[j, step - 1],
                device_id=device, device_id_type=MESH,
            ),
        )

    def m_arrivals(j, step):
        device, other = near(step)
        return (
            pltpu.make_async_remote_copy(
                src_ref=mo.at[j, slot], dst_ref=mo.at[j, other],
                send_sem=m_send.at[j, step - 1], recv_sem=m_recv.at[j, step - 1],
                device_id=device, device_id_type=MESH,
            ),
            pltpu.make_async_remote_copy(
                src_ref=mst.at[j, slot], dst_ref=mst.at[j, other],
                send_sem=n_send.at[j, step - 1], recv_sem=n_recv.at[j, step - 1],
                device_id=device, device_id_type=MESH,
            ),
        )

    def attend(j):
        q_copy(j, 1).wait_recv()
        q_copy(j, 3).wait_recv()
        for p in range(2):
            for way in range(2):
                f_copy(j, p, way).wait_recv()
        for t in range(NY):
            vt[:, t * TOK : (t + 1) * TOK] = kv[j, t, 1].astype(F32).T.astype(BF16)
        queries = qall[j].reshape(QS, HD)
        keys = kv[j, :, 0].reshape(KS, HD)
        scores = lax.dot_general(keys, queries, (((1,), (1,)), ((), ())), preferred_element_type=F32)
        top = jnp.max(scores, axis=0, keepdims=True)
        expo = jnp.exp2(scores - top)
        total = jnp.sum(expo, axis=0, keepdims=True)
        mixed = dot(vt[...], expo.astype(BF16)) / total
        obuf[j] = mixed.T.astype(BF16)
        for i in range(4):
            for r in range(3):
                lanes = slice((2 * i + r) * HD, (2 * i + r + 1) * HD)
                pst[j, i, r : r + 1, :] = top[:, lanes]
                pst[j, i, 3 + r : 4 + r, :] = total[:, lanes]
            pst[j, i, 6:8, :] = jnp.zeros((2, HD), F32)
        for step in (3, 2, 1):
            for copy in m_copies(j, step):
                copy.start()
        mo[j, slot] = obuf[j, pl.ds(pl.multiple_of(slot * TOK, 32), TOK), :]
        mst[j, slot] = pst[j, slot]

    def c_copy(j, zz):
        return pltpu.make_async_remote_copy(
            src_ref=cbuf.at[j, zz], dst_ref=recv_c.at[j, xl, z % 4],
            send_sem=c_send.at[j, zz], recv_sem=c_recv.at[j, xl, z % 4],
            device_id=far(zz, z // 4), device_id_type=MESH,
        )

    def c_own(zz):
        return (xh == c) & (zz == z) & (z // 4 == xl)

    def merge(j):
        for step in range(1, 4):
            for copy in m_arrivals(j, step):
                copy.wait_recv()
        tops = [mst[j, i, 0:3, :] for i in range(4)]
        top = jnp.maximum(jnp.maximum(tops[0], tops[1]), jnp.maximum(tops[2], tops[3]))
        parts = [mst[j, i, 3:6, :] * jnp.exp2(tops[i] - top) for i in range(4)]
        total = (parts[0] + parts[1]) + (parts[2] + parts[3])
        parts = [p / total for p in parts]
        for r in range(3):
            rows = jnp.concatenate([p[r : r + 1] for p in parts] + [jnp.zeros((124, HD), F32)], axis=0)
            wt[r * HD : (r + 1) * HD] = rows.T
        share = wt[pl.ds(pl.multiple_of(slot * 32, 32), TOK), :]
        mixed = share[:, 0:1] * mo[j, 0].astype(F32)
        for i in range(1, 4):
            mixed += share[:, i : i + 1] * mo[j, i].astype(F32)
        mixed = mixed.astype(BF16)
        order = pick((128, 32), lambda r: jnp.where(r % 16 < 4, r // 16 * 4 + r % 16, -1))
        rest = dot(order, mixed[256:288]).astype(BF16)
        for zz in range(NZ):
            cbuf[j, zz, 0:32] = mixed[zz * 32 : zz * 32 + 32]
            cbuf[j, zz, 32:48] = rest[zz * 16 : zz * 16 + 16]

        @pl.loop(0, NZ)
        def _(i):
            zz = (z + outward(i)) % NZ

            @pl.when(c_own(zz))
            def _():
                pltpu.make_async_copy(cbuf.at[j, z], recv_c.at[j, xl, z % 4], c_recv.at[j, xl, z % 4]).start()

            @pl.when(jnp.logical_not(c_own(zz)))
            def _():
                c_copy(j, zz).start()

    sibling = (1 - c, s, xl)

    def s_copy(j):
        return pltpu.make_async_remote_copy(
            src_ref=recv_c.at[j], dst_ref=sib_c.at[j],
            send_sem=s_send.at[j], recv_sem=s_recv.at[j],
            device_id=sibling, device_id_type=MESH,
        )

    def share_out(j):
        for blk in range(2):
            for t in range(4):
                pltpu.make_async_remote_copy(
                    src_ref=cbuf.at[j, 0], dst_ref=recv_c.at[j, blk, t],
                    send_sem=c_send.at[j, 0], recv_sem=c_recv.at[j, blk, t],
                    device_id=sibling, device_id_type=MESH,
                ).wait_recv()
        s_copy(j).start()

    mine = jnp.where(c == 0, GUIDANCE, 1.0 - GUIDANCE)
    theirs = 1.0 - mine

    def d_copy(n):
        src, dst = (dsend.at[n], drecv.at[n]) if n < 3 else (dsend4, drecv4)
        return pltpu.make_async_remote_copy(
            src_ref=src, dst_ref=dst,
            send_sem=d_send.at[n], recv_sem=d_recv.at[n],
            device_id=(c, s, 1 - xl), device_id_type=MESH,
        )

    def project(j):
        s_copy(j).wait_recv()
        for blk in range(2):
            for t in range(4):
                g = mine * recv_c[j, blk, t].astype(F32) + theirs * sib_c[j, blk, t].astype(F32)
                gbuf[blk * 48 : blk * 48 + 48, t * HD : (t + 1) * HD] = g.astype(BF16)
        for t in range(4):
            w_copies[j * 4 + t].wait()
        rest = []
        for n in range(3):
            part = dot(gbuf[...], wv[j, :, n * 512 : (n + 1) * 512])
            if j > 0:
                part += acc[n]
            acc[n] = part
            if j == NJ - 1:
                other = pl.multiple_of((1 - xl) * 48, 16)
                dsend[n] = acc[n, pl.ds(other, MAIN), :].astype(BF16)
                d_copy(n).start()
                rest.append(acc[n, pl.ds(other + MAIN, 8), :][0:REM])
        if j == NJ - 1:
            dsend4[...] = jnp.concatenate(rest + [jnp.zeros_like(rest[0])], axis=0).astype(BF16)
            d_copy(3).start()

    prepare(0)
    pl.semaphore_wait(barrier, jnp.where(xh == c, 21, 22))
    depart(0, 0)
    depart(0, 1)
    depart(0, 2)
    prepare(1)
    depart(1, 0)
    depart(1, 1)
    depart(1, 2)
    prepare(2)
    depart(2, 0)
    depart(2, 1)
    depart(2, 2)
    gather(0, 0)
    gather(0, 1)
    gather(0, 2)
    forward(0, 0)
    forward(0, 1)
    gather(1, 0)
    forward(0, 2)
    gather(1, 1)
    gather(1, 2)
    forward(1, 0)
    attend(0)
    forward(1, 1)
    gather(2, 0)
    gather(2, 1)
    forward(1, 2)
    gather(2, 2)
    forward(2, 0)
    attend(1)
    forward(2, 1)
    forward(2, 2)
    merge(0)
    attend(2)
    merge(1)
    share_out(0)
    project(0)
    merge(2)
    share_out(1)
    project(1)
    share_out(2)
    project(2)

    mine_at = pl.multiple_of(xl * 48, 16)
    for n in range(3):
        d_copy(n).wait_recv()
        full = acc[n, pl.ds(mine_at, MAIN), :] + drecv[n].astype(F32)
        o_ref[0:MAIN, n * 512 : (n + 1) * 512] = full.astype(BF16)
    d_copy(3).wait_recv()
    rest = drecv4[...].astype(F32)
    for n in range(3):
        full = acc[n, pl.ds(mine_at + MAIN, 8), :][0:REM] + rest[n * REM : (n + 1) * REM]
        o_ref[MAIN:ROWS, n * 512 : (n + 1) * 512] = full.astype(BF16)

    for j in range(NJ):
        @pl.loop(0, NZ)
        def _(zz):
            @pl.when(jnp.logical_not(own(zz)))
            def _():
                for p in range(3):
                    a_copy(j, p, zz).wait_send()

            @pl.when(jnp.logical_not(c_own(zz)))
            def _():
                c_copy(j, zz).wait_send()

        for step in range(1, 4):
            q_copy(j, step).wait_send()
            for copy in m_copies(j, step):
                copy.wait_send()
        for p in range(2):
            for way in range(2):
                y_copy(j, p, way).wait_send()
                f_copy(j, p, way).wait_send()
        s_copy(j).wait_send()
    for n in range(4):
        d_copy(n).wait_send()


def shards(query, key, value, out_weight, table):
    hbm = pl.BlockSpec(memory_space=pl.ANY)
    dma = pltpu.SemaphoreType.DMA
    return pl.pallas_call(
        kernel,
        out_shape=jax.ShapeDtypeStruct((ROWS, 1536), BF16),
        in_specs=[hbm] * 5,
        out_specs=pl.BlockSpec(memory_space=pltpu.VMEM),
        scratch_shapes=[
            pltpu.VMEM((ROWS, 3072), BF16),
            pltpu.VMEM((ROWS, 3072), BF16),
            pltpu.VMEM((ROWS, 3072), BF16),
            pltpu.VMEM((2, 40, HD), F32),
            pltpu.VMEM((2, 8, HD), F32),
            pltpu.VMEM((NJ, NZ, 112, HD), BF16),
            pltpu.VMEM((NJ, NZ, 112, HD), BF16),
            pltpu.VMEM((NJ, 4, TOK, HD), BF16),
            pltpu.VMEM((NJ, NY, 2, TOK, HD), BF16),
            pltpu.VMEM((HD, KS), BF16),
            pltpu.VMEM((NJ, QS, HD), BF16),
            pltpu.VMEM((NJ, 4, 8, HD), F32),
            pltpu.VMEM((NJ, 4, TOK, HD), BF16),
            pltpu.VMEM((NJ, 4, 8, HD), F32),
            pltpu.VMEM((3 * HD, HD), F32),
            pltpu.VMEM((NJ, NZ, 48, HD), BF16),
            pltpu.VMEM((NJ, 2, 4, 48, HD), BF16),
            pltpu.VMEM((NJ, 2, 4, 48, HD), BF16),
            pltpu.VMEM((96, 512), BF16),
            pltpu.VMEM((3, 96, 512), F32),
            pltpu.VMEM((3, 32, 512), BF16),
            pltpu.VMEM((3, 32, 512), BF16),
            pltpu.VMEM((16, 512), BF16),
            pltpu.VMEM((16, 512), BF16),
            pltpu.VMEM((NJ, 512, 1536), BF16),
            dma((4,)), dma((NJ, 4)),
            dma((NJ, 3, NZ)), dma((NJ, 3, NZ)),
            dma((NJ, 3)), dma((NJ, 3)),
            dma((NJ, 2, 2)), dma((NJ, 2, 2)),
            dma((NJ, 2, 2)), dma((NJ, 2, 2)),
            dma((NJ, 3)), dma((NJ, 3)),
            dma((NJ, 3)), dma((NJ, 3)),
            dma((NJ, NZ)), dma((NJ, 2, 4)),
            dma((NJ,)), dma((NJ,)),
            dma((4,)), dma((4,)),
        ],
        compiler_params=pltpu.CompilerParams(
            collective_id=0, has_side_effects=True, vmem_limit_bytes=60 * 1024 * 1024
        ),
        cost_estimate=pl.CostEstimate(flops=2_400_000_000, bytes_accessed=8_000_000, transcendentals=4_000_000),
    )(query, key, value, out_weight, table)


def solution(mesh):
    places = mesh.shape["seq"] * mesh.shape["blk"]
    call = jax.shard_map(
        shards,
        mesh=mesh,
        in_specs=(
            P("branch", ("seq", "blk"), None),
            P("branch", ("seq", "blk"), None),
            P("branch", ("seq", "blk"), None),
            P("blk", None),
            P(),
        ),
        out_specs=P(("seq", "blk"), "branch"),
        check_vma=False,
    )

    def run(query, key, value, out_weight):
        return call(query, key, value, out_weight, jnp.asarray(tables(places)))

    return run
```

```python
import functools

import jax
import jax.numpy as jnp
import numpy as np
from jax import lax
from jax.experimental import pallas as pl
from jax.experimental.pallas import tpu as pltpu
from jax.sharding import PartitionSpec as P

HD = 128
GRIDW = 256
GUIDANCE = 4.0
F32 = jnp.float32
BF16 = jnp.bfloat16
MESH = pl.DeviceIdType.MESH

NJ = 3
NZ = 8
NY = 4
ROWS = 36
MAIN = 32
REM = ROWS - MAIN
TOK = NZ * ROWS
QS = 4 * TOK
KS = NY * TOK
PART = (0, 48, 80, 112)
SCALE = float(HD**-0.5 / np.log(2.0))


def tables(places):
    time_dim = HD // 8
    side_dim = (HD - time_dim) // 2
    index = np.arange(side_dim // 2).astype(np.float32)
    freq = np.power(np.float32(10000.0), -2.0 * index / side_dim).astype(np.float32)
    at = np.arange(places * ROWS)
    row = (at // GRIDW).astype(np.float32)[:, None] * freq[None, :]
    col = (at % GRIDW).astype(np.float32)[:, None] * freq[None, :]
    still = np.zeros((places * ROWS, time_dim // 2), np.float32)
    angle = np.repeat(np.concatenate([still, row, col], axis=1), 2, axis=1).astype(np.float64)
    sign = np.where(np.arange(HD) % 2 == 0, -1.0, 1.0)
    both = np.stack([np.cos(angle), np.sin(angle) * sign]).astype(np.float32)
    out = np.zeros((places, 2, 40, HD), np.float32)
    out[:, :, :ROWS] = both.reshape(2, places, ROWS, HD).transpose(1, 0, 2, 3)
    return out


def turn(x, cos, sin):
    even = lax.broadcasted_iota(jnp.int32, x.shape, 1) % 2 == 0
    swapped = jnp.where(even, pltpu.roll(x, HD - 1, 1), pltpu.roll(x, 1, 1))
    return x * cos + swapped * sin


def pick(shape, source):
    row = lax.broadcasted_iota(jnp.int32, shape, 0)
    col = lax.broadcasted_iota(jnp.int32, shape, 1)
    return jnp.where(col == source(row), 1.0, 0.0).astype(BF16)


def outward(i):
    return jnp.where(i % 2 == 1, 4 - (i + 1) // 2, 4 + i // 2)


def dot(a, b):
    return jnp.dot(a, b, preferred_element_type=F32)


def kernel(
    q_hbm, k_hbm, v_hbm, w_ref, tab_ref, o_ref,
    q_ref, k_ref, v_ref, tab, rtab, send_a, recv_a, qall, kv, vt, obuf, pst, mo, mst, wt, cbuf,
    recv_c, sib_c, gbuf, acc, dsend, drecv, dsend4, drecv4, wv,
    in_sem, w_sem, a_send, a_recv, q_send, q_recv, y_send, y_recv, f_send, f_recv,
    m_send, m_recv, n_send, n_recv, c_send, c_recv, s_send, s_recv, d_send, d_recv,
):
    c = lax.axis_index("branch")
    s = lax.axis_index("seq")
    xl = lax.axis_index("blk")
    xh = s // 32
    y = (s // 8) % 4
    z = s % 8
    place = s * 2 + xl
    slot = xl * 2 + c

    def far(zz, blk):
        return (xh, (c * 4 + y) * 8 + zz, blk)

    def ring(step):
        return (c, (xh * 4 + (y + step) % 4) * 8 + z, xl)

    def near(step):
        device = ((c + step) % 2, s, (xl + step // 2) % 2)
        return device, device[2] * 2 + device[0]

    loads = [
        pltpu.make_async_copy(src, dst, in_sem.at[i])
        for i, (src, dst) in enumerate(
            ((tab_ref.at[place], tab), (k_hbm.at[0], k_ref), (q_hbm.at[0], q_ref), (v_hbm.at[0], v_ref))
        )
    ]
    for load in loads:
        load.start()

    barrier = pltpu.get_barrier_semaphore()

    @pl.loop(0, NZ)
    def _(zz):
        for blk in range(2):
            @pl.when(jnp.logical_not((xh == c) & (zz == z) & (xl == blk)))
            def _():
                pl.semaphore_signal(barrier, inc=1, device_id=far(zz, blk), device_id_type=MESH)

    for step in range(1, 4):
        pl.semaphore_signal(barrier, inc=1, device_id=ring(step), device_id_type=MESH)
        pl.semaphore_signal(barrier, inc=1, device_id=near(step)[0], device_id_type=MESH)

    w_copies = []
    for j in range(NJ):
        for t in range(4):
            w_copies.append(
                pltpu.make_async_copy(
                    w_ref.at[pl.ds((t * NJ + j) * HD, HD), pl.ds(pl.multiple_of(c * 1536, 1536), 1536)],
                    wv.at[j, pl.ds(t * HD, HD)],
                    w_sem.at[j, t],
                )
            )

    def weights(j):
        for t in range(4):
            w_copies[j * 4 + t].start()

    def own(zz):
        return (xh == c) & (zz == z)

    def a_copy(j, p, zz):
        rows = pl.ds(PART[p], PART[p + 1] - PART[p])
        return pltpu.make_async_remote_copy(
            src_ref=send_a.at[j, zz, rows], dst_ref=recv_a.at[j, z, rows],
            send_sem=a_send.at[j, p, zz], recv_sem=a_recv.at[j, p, z],
            device_id=far(zz, xl), device_id_type=MESH,
        )

    def a_local(j, p):
        rows = pl.ds(PART[p], PART[p + 1] - PART[p])
        return pltpu.make_async_copy(send_a.at[j, z, rows], recv_a.at[j, z, rows], a_recv.at[j, p, z])

    def a_arrival(j, p, zz):
        rows = pl.ds(PART[p], PART[p + 1] - PART[p])
        return pltpu.make_async_remote_copy(
            src_ref=send_a.at[j, zz, rows], dst_ref=recv_a.at[j, zz, rows],
            send_sem=a_send.at[j, p, zz], recv_sem=a_recv.at[j, p, zz],
            device_id=far(zz, xl), device_id_type=MESH,
        )

    for load in loads:
        load.wait()
    rtab[0, 0:4] = tab[0, 32:36] * SCALE
    rtab[0, 4:8] = tab[0, 32:36]
    rtab[1, 0:4] = tab[1, 32:36] * SCALE
    rtab[1, 4:8] = tab[1, 32:36]

    def prepare(j):
        @pl.loop(0, NZ)
        def _(zz):
            cols = pl.ds(pl.multiple_of((zz * NJ + j) * HD, HD), HD)
            cos, sin = tab[0, 0:MAIN], tab[1, 0:MAIN]
            q = turn(q_ref[0:MAIN, cols].astype(F32), cos * SCALE, sin * SCALE)
            k = turn(k_ref[0:MAIN, cols].astype(F32), cos, sin)
            send_a[j, zz, 0:32] = k.astype(BF16)
            send_a[j, zz, 48:80] = v_ref[0:MAIN, cols]
            send_a[j, zz, 80:112] = q.astype(BF16)
            qk = jnp.concatenate(
                [q_ref[MAIN:ROWS, cols].astype(F32), k_ref[MAIN:ROWS, cols].astype(F32)], axis=0
            )
            v4 = v_ref[MAIN:ROWS, cols].astype(F32)
            rest = jnp.concatenate([turn(qk, rtab[0], rtab[1]), v4, jnp.zeros_like(v4)], axis=0)
            send_a[j, zz, 32:48] = rest.astype(BF16)

    def depart(j, p):
        @pl.loop(0, NZ)
        def _(i):
            zz = (z + outward(i)) % NZ

            @pl.when(own(zz))
            def _():
                a_local(j, p).start()

            @pl.when(jnp.logical_not(own(zz)))
            def _():
                a_copy(j, p, zz).start()

    def y_copy(j, p, way):
        return pltpu.make_async_remote_copy(
            src_ref=kv.at[j, 0, p], dst_ref=kv.at[j, 1 + way, p],
            send_sem=y_send.at[j, p, way], recv_sem=y_recv.at[j, p, way],
            device_id=ring(1 if way == 0 else 3), device_id_type=MESH,
        )

    def f_copy(j, p, way):
        rows = pl.ds(way * 144, 144)
        return pltpu.make_async_remote_copy(
            src_ref=kv.at[j, 1 + way, p, rows], dst_ref=kv.at[j, 3, p, rows],
            send_sem=f_send.at[j, p, way], recv_sem=f_recv.at[j, p, way],
            device_id=ring(1 if way == 0 else 3), device_id_type=MESH,
        )

    def q_copy(j, step):
        which = near(2)[1] if step == 3 else slot
        return pltpu.make_async_remote_copy(
            src_ref=qall.at[j, which], dst_ref=qall.at[j, which],
            send_sem=q_send.at[j, step - 1], recv_sem=q_recv.at[j, step - 1],
            device_id=near(2 if step == 2 else 1)[0], device_id_type=MESH,
        )

    def gather(j, p):
        for zz in range(NZ):
            a_arrival(j, p, zz).wait_recv()
        if p == 0:
            for zz in range(NZ):
                kv[j, 0, 0, zz * 32 : zz * 32 + 32] = recv_a[j, zz, 0:32]
            rest = recv_a[j, :, 32:48, :].reshape(NZ * 16, HD)
            order = pick((96, 128), lambda r: (r % 32) // 4 * 16 + r // 32 * 4 + r % 4)
            rest = dot(order, rest).astype(BF16)
            kv[j, 0, 0, 256:288] = rest[32:64]
            kv[j, 0, 1, 256:288] = rest[64:96]
            qall[j, slot, 256:288] = rest[0:32]
        elif p == 1:
            for zz in range(NZ):
                kv[j, 0, 1, zz * 32 : zz * 32 + 32] = recv_a[j, zz, 48:80]
        else:
            for zz in range(NZ):
                qall[j, slot, zz * 32 : zz * 32 + 32] = recv_a[j, zz, 80:112]
        if p < 2:
            for way in range(2):
                y_copy(j, p, way).start()
        else:
            for step in (2, 1):
                q_copy(j, step).start()

    def forward(j, p):
        if p < 2:
            for way in range(2):
                y_copy(j, p, way).wait_recv()
                f_copy(j, p, way).start()
        else:
            q_copy(j, 2).wait_recv()
            q_copy(j, 3).start()

    def m_copies(j, step):
        device, other = near(step)
        return (
            pltpu.make_async_remote_copy(
                src_ref=obuf.at[j, pl.ds(pl.multiple_of(other * TOK, 32), TOK)], dst_ref=mo.at[j, slot],
                send_sem=m_send.at[j, step - 1], recv_sem=m_recv.at[j, step - 1],
                device_id=device, device_id_type=MESH,
            ),
            pltpu.make_async_remote_copy(
                src_ref=pst.at[j, other], dst_ref=mst.at[j, slot],
                send_sem=n_send.at[j, step - 1], recv_sem=n_recv.at[j, step - 1],
                device_id=device, device_id_type=MESH,
            ),
        )

    def m_arrivals(j, step):
        device, other = near(step)
        return (
            pltpu.make_async_remote_copy(
                src_ref=mo.at[j, slot], dst_ref=mo.at[j, other],
                send_sem=m_send.at[j, step - 1], recv_sem=m_recv.at[j, step - 1],
                device_id=device, device_id_type=MESH,
            ),
            pltpu.make_async_remote_copy(
                src_ref=mst.at[j, slot], dst_ref=mst.at[j, other],
                send_sem=n_send.at[j, step - 1], recv_sem=n_recv.at[j, step - 1],
                device_id=device, device_id_type=MESH,
            ),
        )

    def attend_rows(j, first, count):
        queries = qall[j, pl.ds(first, count)].reshape(count * TOK, HD)
        keys = kv[j, :, 0].reshape(KS, HD)
        scores = lax.dot_general(keys, queries, (((1,), (1,)), ((), ())), preferred_element_type=F32)
        top = jnp.max(scores, axis=0, keepdims=True)
        expo = jnp.exp2(scores - top)
        total = jnp.sum(expo, axis=0, keepdims=True)
        mixed = dot(vt[...], expo.astype(BF16)) / total
        obuf[j, pl.ds(pl.multiple_of(first * TOK, 32), count * TOK)] = mixed.T.astype(BF16)
        for i in range(count):
            for r in range(3):
                lanes = slice((2 * i + r) * HD, min((2 * i + r + 1) * HD, count * TOK))
                wide = slice(0, lanes.stop - lanes.start)
                pst[j, first + i, r : r + 1, wide] = top[:, lanes]
                pst[j, first + i, 3 + r : 4 + r, wide] = total[:, lanes]

    def attend(j):
        q_copy(j, 1).wait_recv()
        q_copy(j, 3).wait_recv()
        for p in range(2):
            for way in range(2):
                f_copy(j, p, way).wait_recv()
        for t in range(NY):
            vt[:, t * TOK : (t + 1) * TOK] = kv[j, t, 1].astype(F32).T.astype(BF16)
        pst[j] = jnp.ones((4, 8, HD), F32)
        if j < NJ - 1:
            attend_rows(j, 0, 4)
        else:
            attend_rows(j, (1 - xl) * 2, 2)
        for step in (3, 2):
            for copy in m_copies(j, step):
                copy.start()
        if j == NJ - 1:
            attend_rows(j, xl * 2, 2)
        for copy in m_copies(j, 1):
            copy.start()
        mo[j, slot] = obuf[j, pl.ds(pl.multiple_of(slot * TOK, 32), TOK), :]
        mst[j, slot] = pst[j, slot]

    def c_copy(j, zz):
        return pltpu.make_async_remote_copy(
            src_ref=cbuf.at[j, zz], dst_ref=recv_c.at[j, xl, z % 4],
            send_sem=c_send.at[j, zz], recv_sem=c_recv.at[j, xl, z % 4],
            device_id=far(zz, z // 4), device_id_type=MESH,
        )

    def c_own(zz):
        return (xh == c) & (zz == z) & (z // 4 == xl)

    def merge(j):
        for step in range(1, 4):
            for copy in m_arrivals(j, step):
                copy.wait_recv()
        tops = [mst[j, i, 0:3, :] for i in range(4)]
        top = jnp.maximum(jnp.maximum(tops[0], tops[1]), jnp.maximum(tops[2], tops[3]))
        parts = [mst[j, i, 3:6, :] * jnp.exp2(tops[i] - top) for i in range(4)]
        total = (parts[0] + parts[1]) + (parts[2] + parts[3])
        parts = [p / total for p in parts]
        for r in range(3):
            rows = jnp.concatenate([p[r : r + 1] for p in parts] + [jnp.zeros((124, HD), F32)], axis=0)
            wt[r * HD : (r + 1) * HD] = rows.T
        at = slot if j < NJ - 1 else c
        share = wt[pl.ds(pl.multiple_of(at * 32, 32), TOK), :]
        mixed = share[:, 0:1] * mo[j, 0].astype(F32)
        for i in range(1, 4):
            mixed += share[:, i : i + 1] * mo[j, i].astype(F32)
        mixed = mixed.astype(BF16)
        order = pick((128, 32), lambda r: jnp.where(r % 16 < 4, r // 16 * 4 + r % 16, -1))
        rest = dot(order, mixed[256:288]).astype(BF16)
        for zz in range(NZ):
            cbuf[j, zz, 0:32] = mixed[zz * 32 : zz * 32 + 32]
            cbuf[j, zz, 32:48] = rest[zz * 16 : zz * 16 + 16]

        @pl.loop(0, NZ)
        def _(i):
            zz = (z + outward(i)) % NZ

            @pl.when(c_own(zz))
            def _():
                pltpu.make_async_copy(cbuf.at[j, z], recv_c.at[j, xl, z % 4], c_recv.at[j, xl, z % 4]).start()

            @pl.when(jnp.logical_not(c_own(zz)))
            def _():
                c_copy(j, zz).start()

    sibling = (1 - c, s, xl)

    def s_copy(j):
        return pltpu.make_async_remote_copy(
            src_ref=recv_c.at[j], dst_ref=sib_c.at[j],
            send_sem=s_send.at[j], recv_sem=s_recv.at[j],
            device_id=sibling, device_id_type=MESH,
        )

    def share_out(j):
        for blk in range(2):
            for t in range(4):
                pltpu.make_async_remote_copy(
                    src_ref=cbuf.at[j, 0], dst_ref=recv_c.at[j, blk, t],
                    send_sem=c_send.at[j, 0], recv_sem=c_recv.at[j, blk, t],
                    device_id=sibling, device_id_type=MESH,
                ).wait_recv()
        s_copy(j).start()

    mine = jnp.where(c == 0, GUIDANCE, 1.0 - GUIDANCE)
    theirs = 1.0 - mine

    def d_copy(n):
        src, dst = (dsend.at[n], drecv.at[n]) if n < 3 else (dsend4, drecv4)
        return pltpu.make_async_remote_copy(
            src_ref=src, dst_ref=dst,
            send_sem=d_send.at[n], recv_sem=d_recv.at[n],
            device_id=(c, s, 1 - xl), device_id_type=MESH,
        )

    def project(j):
        s_copy(j).wait_recv()
        for blk in range(2):
            for t in range(4):
                g = mine * recv_c[j, blk, t].astype(F32) + theirs * sib_c[j, blk, t].astype(F32)
                gbuf[blk * 48 : blk * 48 + 48, t * HD : (t + 1) * HD] = g.astype(BF16)
        for t in range(4):
            w_copies[j * 4 + t].wait()
        rest = []
        for n in range(3):
            part = dot(gbuf[...], wv[j, :, n * 512 : (n + 1) * 512])
            if j > 0:
                part += acc[n]
            acc[n] = part
            if j == NJ - 1:
                other = pl.multiple_of((1 - xl) * 48, 16)
                dsend[n] = acc[n, pl.ds(other, MAIN), :].astype(BF16)
                d_copy(n).start()
                rest.append(acc[n, pl.ds(other + MAIN, 8), :][0:REM])
        if j == NJ - 1:
            dsend4[...] = jnp.concatenate(rest + [jnp.zeros_like(rest[0])], axis=0).astype(BF16)
            d_copy(3).start()

    prepare(0)
    pl.semaphore_wait(barrier, jnp.where(xh == c, 21, 22))
    depart(0, 0)
    depart(0, 1)
    depart(0, 2)
    prepare(1)
    depart(1, 0)
    depart(1, 1)
    depart(1, 2)
    prepare(2)
    depart(2, 0)
    depart(2, 1)
    depart(2, 2)
    gather(0, 0)
    gather(0, 1)
    gather(0, 2)
    forward(0, 0)
    forward(0, 1)
    gather(1, 0)
    forward(0, 2)
    gather(1, 1)
    gather(1, 2)
    forward(1, 0)
    attend(0)
    forward(1, 1)
    gather(2, 0)
    gather(2, 1)
    forward(1, 2)
    gather(2, 2)
    forward(2, 0)
    attend(1)
    forward(2, 1)
    forward(2, 2)
    weights(0)
    merge(0)
    attend(2)
    weights(1)
    weights(2)
    merge(1)
    share_out(0)
    project(0)
    merge(2)
    share_out(1)
    project(1)
    share_out(2)
    project(2)

    mine_at = pl.multiple_of(xl * 48, 16)
    for n in range(3):
        d_copy(n).wait_recv()
        full = acc[n, pl.ds(mine_at, MAIN), :] + drecv[n].astype(F32)
        o_ref[0:MAIN, n * 512 : (n + 1) * 512] = full.astype(BF16)
    d_copy(3).wait_recv()
    rest = drecv4[...].astype(F32)
    for n in range(3):
        full = acc[n, pl.ds(mine_at + MAIN, 8), :][0:REM] + rest[n * REM : (n + 1) * REM]
        o_ref[MAIN:ROWS, n * 512 : (n + 1) * 512] = full.astype(BF16)

    for j in range(NJ):
        @pl.loop(0, NZ)
        def _(zz):
            @pl.when(jnp.logical_not(own(zz)))
            def _():
                for p in range(3):
                    a_copy(j, p, zz).wait_send()

            @pl.when(jnp.logical_not(c_own(zz)))
            def _():
                c_copy(j, zz).wait_send()

        for step in range(1, 4):
            q_copy(j, step).wait_send()
            for copy in m_copies(j, step):
                copy.wait_send()
        for p in range(2):
            for way in range(2):
                y_copy(j, p, way).wait_send()
                f_copy(j, p, way).wait_send()
        s_copy(j).wait_send()
    for n in range(4):
        d_copy(n).wait_send()


def shards(query, key, value, out_weight, table):
    hbm = pl.BlockSpec(memory_space=pl.ANY)
    dma = pltpu.SemaphoreType.DMA
    return pl.pallas_call(
        kernel,
        out_shape=pltpu.VMEM((ROWS, 1536), BF16),
        in_specs=[hbm] * 5,
        out_specs=pl.BlockSpec(memory_space=pltpu.VMEM),
        scratch_shapes=[
            pltpu.VMEM((ROWS, 3072), BF16),
            pltpu.VMEM((ROWS, 3072), BF16),
            pltpu.VMEM((ROWS, 3072), BF16),
            pltpu.VMEM((2, 40, HD), F32),
            pltpu.VMEM((2, 8, HD), F32),
            pltpu.VMEM((NJ, NZ, 112, HD), BF16),
            pltpu.VMEM((NJ, NZ, 112, HD), BF16),
            pltpu.VMEM((NJ, 4, TOK, HD), BF16),
            pltpu.VMEM((NJ, NY, 2, TOK, HD), BF16),
            pltpu.VMEM((HD, KS), BF16),
            pltpu.VMEM((NJ, QS, HD), BF16),
            pltpu.VMEM((NJ, 4, 8, HD), F32),
            pltpu.VMEM((NJ, 4, TOK, HD), BF16),
            pltpu.VMEM((NJ, 4, 8, HD), F32),
            pltpu.VMEM((3 * HD, HD), F32),
            pltpu.VMEM((NJ, NZ, 48, HD), BF16),
            pltpu.VMEM((NJ, 2, 4, 48, HD), BF16),
            pltpu.VMEM((NJ, 2, 4, 48, HD), BF16),
            pltpu.VMEM((96, 512), BF16),
            pltpu.VMEM((3, 96, 512), F32),
            pltpu.VMEM((3, 32, 512), BF16),
            pltpu.VMEM((3, 32, 512), BF16),
            pltpu.VMEM((16, 512), BF16),
            pltpu.VMEM((16, 512), BF16),
            pltpu.VMEM((NJ, 512, 1536), BF16),
            dma((4,)), dma((NJ, 4)),
            dma((NJ, 3, NZ)), dma((NJ, 3, NZ)),
            dma((NJ, 3)), dma((NJ, 3)),
            dma((NJ, 2, 2)), dma((NJ, 2, 2)),
            dma((NJ, 2, 2)), dma((NJ, 2, 2)),
            dma((NJ, 3)), dma((NJ, 3)),
            dma((NJ, 3)), dma((NJ, 3)),
            dma((NJ, NZ)), dma((NJ, 2, 4)),
            dma((NJ,)), dma((NJ,)),
            dma((4,)), dma((4,)),
        ],
        compiler_params=pltpu.CompilerParams(
            collective_id=0, has_side_effects=True, vmem_limit_bytes=60 * 1024 * 1024
        ),
        cost_estimate=pl.CostEstimate(flops=2_400_000_000, bytes_accessed=8_000_000, transcendentals=4_000_000),
    )(query, key, value, out_weight, table)


def solution(mesh):
    places = mesh.shape["seq"] * mesh.shape["blk"]
    call = jax.shard_map(
        shards,
        mesh=mesh,
        in_specs=(
            P("branch", ("seq", "blk"), None),
            P("branch", ("seq", "blk"), None),
            P("branch", ("seq", "blk"), None),
            P("blk", None),
            P(),
        ),
        out_specs=P(("seq", "blk"), "branch"),
        check_vma=False,
    )

    def run(query, key, value, out_weight):
        return call(query, key, value, out_weight, jnp.asarray(tables(places)))

    return run
```

```python
import functools

import jax
import jax.numpy as jnp
import numpy as np
from jax import lax
from jax.experimental import pallas as pl
from jax.experimental.pallas import tpu as pltpu
from jax.sharding import PartitionSpec as P

HD = 128
GRIDW = 256
GUIDANCE = 4.0
F32 = jnp.float32
BF16 = jnp.bfloat16
MESH = pl.DeviceIdType.MESH

NJ = 3
NZ = 8
NY = 4
ROWS = 36
MAIN = 32
REM = ROWS - MAIN
TOK = NZ * ROWS
QS = 4 * TOK
KS = NY * TOK
PART = (0, 48, 80, 112)
SCALE = float(HD**-0.5 / np.log(2.0))


def tables(places):
    time_dim = HD // 8
    side_dim = (HD - time_dim) // 2
    index = np.arange(side_dim // 2).astype(np.float32)
    freq = np.power(np.float32(10000.0), -2.0 * index / side_dim).astype(np.float32)
    at = np.arange(places * ROWS)
    row = (at // GRIDW).astype(np.float32)[:, None] * freq[None, :]
    col = (at % GRIDW).astype(np.float32)[:, None] * freq[None, :]
    still = np.zeros((places * ROWS, time_dim // 2), np.float32)
    angle = np.repeat(np.concatenate([still, row, col], axis=1), 2, axis=1).astype(np.float64)
    sign = np.where(np.arange(HD) % 2 == 0, -1.0, 1.0)
    both = np.stack([np.cos(angle), np.sin(angle) * sign]).astype(np.float32)
    out = np.zeros((places, 2, 40, HD), np.float32)
    out[:, :, :ROWS] = both.reshape(2, places, ROWS, HD).transpose(1, 0, 2, 3)
    return out


def turn(x, cos, sin):
    even = lax.broadcasted_iota(jnp.int32, x.shape, 1) % 2 == 0
    swapped = jnp.where(even, pltpu.roll(x, HD - 1, 1), pltpu.roll(x, 1, 1))
    return x * cos + swapped * sin


def pick(shape, source):
    row = lax.broadcasted_iota(jnp.int32, shape, 0)
    col = lax.broadcasted_iota(jnp.int32, shape, 1)
    return jnp.where(col == source(row), 1.0, 0.0).astype(BF16)


def outward(i):
    return jnp.where(i % 2 == 1, 4 - (i + 1) // 2, 4 + i // 2)


def dot(a, b):
    return jnp.dot(a, b, preferred_element_type=F32)


def kernel(
    q_hbm, k_hbm, v_hbm, w_ref, tab_ref, o_ref,
    q_ref, k_ref, v_ref, tab, rtab, send_a, recv_a, qall, kv, vt, obuf, pst, mo, mst, wt, cbuf,
    recv_c, sib_c, gbuf, acc, dsend, drecv, dsend4, drecv4, wv,
    in_sem, w_sem, a_send, a_recv, q_send, q_recv, y_send, y_recv,
    m_send, m_recv, n_send, n_recv, c_send, c_recv, s_send, s_recv, d_send, d_recv,
):
    c = lax.axis_index("branch")
    s = lax.axis_index("seq")
    xl = lax.axis_index("blk")
    xh = s // 32
    y = (s // 8) % 4
    z = s % 8
    place = s * 2 + xl
    slot = xl * 2 + c

    def far(zz, blk):
        return (xh, (c * 4 + y) * 8 + zz, blk)

    def ring(step):
        return (c, (xh * 4 + (y + step) % 4) * 8 + z, xl)

    def near(step):
        device = ((c + step) % 2, s, (xl + step // 2) % 2)
        return device, device[2] * 2 + device[0]

    loads = [
        pltpu.make_async_copy(src, dst, in_sem.at[i])
        for i, (src, dst) in enumerate(
            ((tab_ref.at[place], tab), (k_hbm.at[0], k_ref), (q_hbm.at[0], q_ref), (v_hbm.at[0], v_ref))
        )
    ]
    for load in loads:
        load.start()

    barrier = pltpu.get_barrier_semaphore()

    @pl.loop(0, NZ)
    def _(zz):
        for blk in range(2):
            @pl.when(jnp.logical_not((xh == c) & (zz == z) & (xl == blk)))
            def _():
                pl.semaphore_signal(barrier, inc=1, device_id=far(zz, blk), device_id_type=MESH)

    for step in range(1, 4):
        pl.semaphore_signal(barrier, inc=1, device_id=ring(step), device_id_type=MESH)
        pl.semaphore_signal(barrier, inc=1, device_id=near(step)[0], device_id_type=MESH)

    w_copies = []
    for j in range(NJ):
        for t in range(4):
            w_copies.append(
                pltpu.make_async_copy(
                    w_ref.at[pl.ds((t * NJ + j) * HD, HD), pl.ds(pl.multiple_of(c * 1536, 1536), 1536)],
                    wv.at[j, pl.ds(t * HD, HD)],
                    w_sem.at[j, t],
                )
            )

    def weights(j):
        for t in range(4):
            w_copies[j * 4 + t].start()

    def own(zz):
        return (xh == c) & (zz == z)

    def a_copy(j, p, zz):
        rows = pl.ds(PART[p], PART[p + 1] - PART[p])
        return pltpu.make_async_remote_copy(
            src_ref=send_a.at[j, zz, rows], dst_ref=recv_a.at[j, z, rows],
            send_sem=a_send.at[j, p, zz], recv_sem=a_recv.at[j, p, z],
            device_id=far(zz, xl), device_id_type=MESH,
        )

    def a_local(j, p):
        rows = pl.ds(PART[p], PART[p + 1] - PART[p])
        return pltpu.make_async_copy(send_a.at[j, z, rows], recv_a.at[j, z, rows], a_recv.at[j, p, z])

    def a_arrival(j, p, zz):
        rows = pl.ds(PART[p], PART[p + 1] - PART[p])
        return pltpu.make_async_remote_copy(
            src_ref=send_a.at[j, zz, rows], dst_ref=recv_a.at[j, zz, rows],
            send_sem=a_send.at[j, p, zz], recv_sem=a_recv.at[j, p, zz],
            device_id=far(zz, xl), device_id_type=MESH,
        )

    for load in loads:
        load.wait()
    rtab[0, 0:4] = tab[0, 32:36] * SCALE
    rtab[0, 4:8] = tab[0, 32:36]
    rtab[1, 0:4] = tab[1, 32:36] * SCALE
    rtab[1, 4:8] = tab[1, 32:36]

    def prepare(j):
        @pl.loop(0, NZ)
        def _(zz):
            cols = pl.ds(pl.multiple_of((zz * NJ + j) * HD, HD), HD)
            cos, sin = tab[0, 0:MAIN], tab[1, 0:MAIN]
            q = turn(q_ref[0:MAIN, cols].astype(F32), cos * SCALE, sin * SCALE)
            k = turn(k_ref[0:MAIN, cols].astype(F32), cos, sin)
            send_a[j, zz, 0:32] = k.astype(BF16)
            send_a[j, zz, 48:80] = v_ref[0:MAIN, cols]
            send_a[j, zz, 80:112] = q.astype(BF16)
            qk = jnp.concatenate(
                [q_ref[MAIN:ROWS, cols].astype(F32), k_ref[MAIN:ROWS, cols].astype(F32)], axis=0
            )
            v4 = v_ref[MAIN:ROWS, cols].astype(F32)
            rest = jnp.concatenate([turn(qk, rtab[0], rtab[1]), v4, jnp.zeros_like(v4)], axis=0)
            send_a[j, zz, 32:48] = rest.astype(BF16)

    def depart(j, p):
        @pl.loop(0, NZ)
        def _(i):
            zz = (z + outward(i)) % NZ

            @pl.when(own(zz))
            def _():
                a_local(j, p).start()

            @pl.when(jnp.logical_not(own(zz)))
            def _():
                a_copy(j, p, zz).start()

    def y_copy(j, p, way):
        return pltpu.make_async_remote_copy(
            src_ref=kv.at[j, 0, p], dst_ref=kv.at[j, 1 + way, p],
            send_sem=y_send.at[j, p, way], recv_sem=y_recv.at[j, p, way],
            device_id=ring((1, 3, 2)[way]), device_id_type=MESH,
        )

    def q_copy(j, step):
        return pltpu.make_async_remote_copy(
            src_ref=qall.at[j, slot], dst_ref=qall.at[j, slot],
            send_sem=q_send.at[j, step - 1], recv_sem=q_recv.at[j, step - 1],
            device_id=near(step)[0], device_id_type=MESH,
        )

    def gather(j, p):
        for zz in range(NZ):
            a_arrival(j, p, zz).wait_recv()
        if p == 0:
            for zz in range(NZ):
                kv[j, 0, 0, zz * 32 : zz * 32 + 32] = recv_a[j, zz, 0:32]
            rest = recv_a[j, :, 32:48, :].reshape(NZ * 16, HD)
            order = pick((96, 128), lambda r: (r % 32) // 4 * 16 + r // 32 * 4 + r % 4)
            rest = dot(order, rest).astype(BF16)
            kv[j, 0, 0, 256:288] = rest[32:64]
            kv[j, 0, 1, 256:288] = rest[64:96]
            qall[j, slot, 256:288] = rest[0:32]
        elif p == 1:
            for zz in range(NZ):
                kv[j, 0, 1, zz * 32 : zz * 32 + 32] = recv_a[j, zz, 48:80]
        else:
            for zz in range(NZ):
                qall[j, slot, zz * 32 : zz * 32 + 32] = recv_a[j, zz, 80:112]
        if p < 2:
            for way in (2, 0, 1):
                y_copy(j, p, way).start()
        else:
            for step in (3, 2, 1):
                q_copy(j, step).start()

    def pieces(j, step):
        return ((128, 160), (0, 128)) if j == NJ - 1 and step > 1 else ((0, TOK),)

    def m_copy(j, step, piece):
        device, other = near(step)
        first, rows = pieces(j, step)[piece]
        return pltpu.make_async_remote_copy(
            src_ref=obuf.at[j, pl.ds(pl.multiple_of(other * TOK + first, 32), rows)],
            dst_ref=mo.at[j, slot, pl.ds(first, rows)],
            send_sem=m_send.at[j, step - 1, piece], recv_sem=m_recv.at[j, step - 1, piece],
            device_id=device, device_id_type=MESH,
        )

    def m_arrival(j, step, piece):
        device, other = near(step)
        rows = pl.ds(*pieces(j, step)[piece])
        return pltpu.make_async_remote_copy(
            src_ref=mo.at[j, slot, rows], dst_ref=mo.at[j, other, rows],
            send_sem=m_send.at[j, step - 1, piece], recv_sem=m_recv.at[j, step - 1, piece],
            device_id=device, device_id_type=MESH,
        )

    def n_copy(j, step):
        device, other = near(step)
        return pltpu.make_async_remote_copy(
            src_ref=pst.at[j, other], dst_ref=mst.at[j, slot],
            send_sem=n_send.at[j, step - 1], recv_sem=n_recv.at[j, step - 1],
            device_id=device, device_id_type=MESH,
        )

    def n_arrival(j, step):
        device, other = near(step)
        return pltpu.make_async_remote_copy(
            src_ref=mst.at[j, slot], dst_ref=mst.at[j, other],
            send_sem=n_send.at[j, step - 1], recv_sem=n_recv.at[j, step - 1],
            device_id=device, device_id_type=MESH,
        )

    def attend_rows(j, first, count):
        queries = qall[j, pl.ds(first, count)].reshape(count * TOK, HD)
        keys = kv[j, :, 0].reshape(KS, HD)
        scores = lax.dot_general(keys, queries, (((1,), (1,)), ((), ())), preferred_element_type=F32)
        top = jnp.max(scores, axis=0, keepdims=True)
        expo = jnp.exp2(scores - top)
        total = jnp.sum(expo, axis=0, keepdims=True)
        mixed = dot(vt[...], expo.astype(BF16)) / total
        obuf[j, pl.ds(pl.multiple_of(first * TOK, 32), count * TOK)] = mixed.T.astype(BF16)
        for i in range(count):
            for r in range(3):
                lanes = slice((2 * i + r) * HD, min((2 * i + r + 1) * HD, count * TOK))
                wide = slice(0, lanes.stop - lanes.start)
                pst[j, first + i, r : r + 1, wide] = top[:, lanes]
                pst[j, first + i, 3 + r : 4 + r, wide] = total[:, lanes]

    def attend(j):
        for step in range(1, 4):
            q_copy(j, step).wait_recv()
        for p in range(2):
            for way in range(3):
                y_copy(j, p, way).wait_recv()
        for t in range(NY):
            vt[:, t * TOK : (t + 1) * TOK] = kv[j, t, 1].astype(F32).T.astype(BF16)
        pst[j] = jnp.ones((4, 8, HD), F32)
        last = j == NJ - 1
        if last:
            attend_rows(j, (1 - xl) * 2, 2)
        else:
            attend_rows(j, 0, 4)
        for step in (3, 2):
            n_copy(j, step).start()
            m_copy(j, step, 0).start()
        if last:
            attend_rows(j, xl * 2, 2)
        n_copy(j, 1).start()
        m_copy(j, 1, 0).start()
        if last:
            for step in (3, 2):
                m_copy(j, step, 1).start()
        mo[j, slot] = obuf[j, pl.ds(pl.multiple_of(slot * TOK, 32), TOK), :]
        mst[j, slot] = pst[j, slot]

    def c_copy(j, zz):
        return pltpu.make_async_remote_copy(
            src_ref=cbuf.at[j, zz], dst_ref=recv_c.at[j, xl, z % 4],
            send_sem=c_send.at[j, zz], recv_sem=c_recv.at[j, xl, z % 4],
            device_id=far(zz, z // 4), device_id_type=MESH,
        )

    def c_own(zz):
        return (xh == c) & (zz == z) & (z // 4 == xl)

    def shares(j):
        for step in range(1, 4):
            n_arrival(j, step).wait_recv()
        tops = [mst[j, i, 0:3, :] for i in range(4)]
        top = jnp.maximum(jnp.maximum(tops[0], tops[1]), jnp.maximum(tops[2], tops[3]))
        parts = [mst[j, i, 3:6, :] * jnp.exp2(tops[i] - top) for i in range(4)]
        total = (parts[0] + parts[1]) + (parts[2] + parts[3])
        parts = [p / total for p in parts]
        for r in range(3):
            rows = jnp.concatenate([p[r : r + 1] for p in parts] + [jnp.zeros((124, HD), F32)], axis=0)
            wt[r * HD : (r + 1) * HD] = rows.T

    def merge_rows(j, first, rows):
        at = c if j == NJ - 1 else slot
        share = wt[pl.ds(pl.multiple_of(at * 32 + first, 32), rows), :]
        mixed = share[:, 0:1] * mo[j, 0, first : first + rows].astype(F32)
        for i in range(1, 4):
            mixed += share[:, i : i + 1] * mo[j, i, first : first + rows].astype(F32)
        mixed = mixed.astype(BF16)
        for n in range(min(rows, 256 - first) // MAIN):
            cbuf[j, first // MAIN + n, 0:32] = mixed[n * MAIN : (n + 1) * MAIN]
        if first + rows == TOK:
            order = pick((128, 32), lambda r: jnp.where(r % 16 < 4, r // 16 * 4 + r % 16, -1))
            rest = dot(order, mixed[256 - first : TOK - first]).astype(BF16)
            for zz in range(NZ):
                cbuf[j, zz, 32:48] = rest[zz * 16 : zz * 16 + 16]

    def c_depart(j, zz):
        @pl.when(c_own(zz))
        def _():
            pltpu.make_async_copy(cbuf.at[j, z], recv_c.at[j, xl, z % 4], c_recv.at[j, xl, z % 4]).start()

        @pl.when(jnp.logical_not(c_own(zz)))
        def _():
            c_copy(j, zz).start()

    def merge(j):
        for step in range(1, 4):
            m_arrival(j, step, 0).wait_recv()
        shares(j)
        if j < NJ - 1:
            merge_rows(j, 0, TOK)
            pl.loop(0, NZ)(lambda i: c_depart(j, (z + outward(i)) % NZ))
        else:
            merge_rows(j, 128, 160)
            pl.loop(0, 4)(lambda i: c_depart(j, 4 + (z + i) % 4))
            for step in (3, 2):
                m_arrival(j, step, 1).wait_recv()
            merge_rows(j, 0, 128)
            pl.loop(0, 4)(lambda i: c_depart(j, (z + i) % 4))

    sibling = (1 - c, s, xl)

    def s_copy(j):
        return pltpu.make_async_remote_copy(
            src_ref=recv_c.at[j], dst_ref=sib_c.at[j],
            send_sem=s_send.at[j], recv_sem=s_recv.at[j],
            device_id=sibling, device_id_type=MESH,
        )

    def share_out(j):
        for blk in range(2):
            for t in range(4):
                pltpu.make_async_remote_copy(
                    src_ref=cbuf.at[j, 0], dst_ref=recv_c.at[j, blk, t],
                    send_sem=c_send.at[j, 0], recv_sem=c_recv.at[j, blk, t],
                    device_id=sibling, device_id_type=MESH,
                ).wait_recv()
        s_copy(j).start()

    mine = jnp.where(c == 0, GUIDANCE, 1.0 - GUIDANCE)
    theirs = 1.0 - mine

    def d_copy(n):
        src, dst = (dsend.at[n], drecv.at[n]) if n < 3 else (dsend4, drecv4)
        return pltpu.make_async_remote_copy(
            src_ref=src, dst_ref=dst,
            send_sem=d_send.at[n], recv_sem=d_recv.at[n],
            device_id=(c, s, 1 - xl), device_id_type=MESH,
        )

    def project(j):
        s_copy(j).wait_recv()
        for blk in range(2):
            for t in range(4):
                g = mine * recv_c[j, blk, t].astype(F32) + theirs * sib_c[j, blk, t].astype(F32)
                gbuf[blk * 48 : blk * 48 + 48, t * HD : (t + 1) * HD] = g.astype(BF16)
        for t in range(4):
            w_copies[j * 4 + t].wait()
        rest = []
        for n in range(3):
            part = dot(gbuf[...], wv[j, :, n * 512 : (n + 1) * 512])
            if j > 0:
                part += acc[n]
            acc[n] = part
            if j == NJ - 1:
                other = pl.multiple_of((1 - xl) * 48, 16)
                dsend[n] = acc[n, pl.ds(other, MAIN), :].astype(BF16)
                d_copy(n).start()
                rest.append(acc[n, pl.ds(other + MAIN, 8), :][0:REM])
        if j == NJ - 1:
            dsend4[...] = jnp.concatenate(rest + [jnp.zeros_like(rest[0])], axis=0).astype(BF16)
            d_copy(3).start()

    prepare(0)
    pl.semaphore_wait(barrier, jnp.where(xh == c, 21, 22))
    depart(0, 0)
    depart(0, 1)
    depart(0, 2)
    prepare(1)
    depart(1, 0)
    depart(1, 1)
    depart(1, 2)
    prepare(2)
    depart(2, 0)
    depart(2, 1)
    depart(2, 2)
    gather(0, 0)
    gather(0, 1)
    gather(0, 2)
    gather(1, 0)
    gather(1, 1)
    gather(1, 2)
    attend(0)
    gather(2, 0)
    gather(2, 1)
    gather(2, 2)
    attend(1)
    weights(0)
    merge(0)
    attend(2)
    weights(1)
    weights(2)
    merge(1)
    share_out(0)
    project(0)
    merge(2)
    share_out(1)
    project(1)
    share_out(2)
    project(2)

    mine_at = pl.multiple_of(xl * 48, 16)
    for n in range(3):
        d_copy(n).wait_recv()
        full = acc[n, pl.ds(mine_at, MAIN), :] + drecv[n].astype(F32)
        o_ref[0:MAIN, n * 512 : (n + 1) * 512] = full.astype(BF16)
    d_copy(3).wait_recv()
    rest = drecv4[...].astype(F32)
    for n in range(3):
        full = acc[n, pl.ds(mine_at + MAIN, 8), :][0:REM] + rest[n * REM : (n + 1) * REM]
        o_ref[MAIN:ROWS, n * 512 : (n + 1) * 512] = full.astype(BF16)

    for j in range(NJ):
        @pl.loop(0, NZ)
        def _(zz):
            @pl.when(jnp.logical_not(own(zz)))
            def _():
                for p in range(3):
                    a_copy(j, p, zz).wait_send()

            @pl.when(jnp.logical_not(c_own(zz)))
            def _():
                c_copy(j, zz).wait_send()

        for step in range(1, 4):
            q_copy(j, step).wait_send()
            n_copy(j, step).wait_send()
            for piece in range(len(pieces(j, step))):
                m_copy(j, step, piece).wait_send()
        for p in range(2):
            for way in range(3):
                y_copy(j, p, way).wait_send()
        s_copy(j).wait_send()
    for n in range(4):
        d_copy(n).wait_send()


def shards(query, key, value, out_weight, table):
    hbm = pl.BlockSpec(memory_space=pl.ANY)
    dma = pltpu.SemaphoreType.DMA
    return pl.pallas_call(
        kernel,
        out_shape=pltpu.VMEM((ROWS, 1536), BF16),
        in_specs=[hbm] * 5,
        out_specs=pl.BlockSpec(memory_space=pltpu.VMEM),
        scratch_shapes=[
            pltpu.VMEM((ROWS, 3072), BF16),
            pltpu.VMEM((ROWS, 3072), BF16),
            pltpu.VMEM((ROWS, 3072), BF16),
            pltpu.VMEM((2, 40, HD), F32),
            pltpu.VMEM((2, 8, HD), F32),
            pltpu.VMEM((NJ, NZ, 112, HD), BF16),
            pltpu.VMEM((NJ, NZ, 112, HD), BF16),
            pltpu.VMEM((NJ, 4, TOK, HD), BF16),
            pltpu.VMEM((NJ, NY, 2, TOK, HD), BF16),
            pltpu.VMEM((HD, KS), BF16),
            pltpu.VMEM((NJ, QS, HD), BF16),
            pltpu.VMEM((NJ, 4, 8, HD), F32),
            pltpu.VMEM((NJ, 4, TOK, HD), BF16),
            pltpu.VMEM((NJ, 4, 8, HD), F32),
            pltpu.VMEM((3 * HD, HD), F32),
            pltpu.VMEM((NJ, NZ, 48, HD), BF16),
            pltpu.VMEM((NJ, 2, 4, 48, HD), BF16),
            pltpu.VMEM((NJ, 2, 4, 48, HD), BF16),
            pltpu.VMEM((96, 512), BF16),
            pltpu.VMEM((3, 96, 512), F32),
            pltpu.VMEM((3, 32, 512), BF16),
            pltpu.VMEM((3, 32, 512), BF16),
            pltpu.VMEM((16, 512), BF16),
            pltpu.VMEM((16, 512), BF16),
            pltpu.VMEM((NJ, 512, 1536), BF16),
            dma((4,)), dma((NJ, 4)),
            dma((NJ, 3, NZ)), dma((NJ, 3, NZ)),
            dma((NJ, 3)), dma((NJ, 3)),
            dma((NJ, 2, 3)), dma((NJ, 2, 3)),
            dma((NJ, 3, 2)), dma((NJ, 3, 2)),
            dma((NJ, 3)), dma((NJ, 3)),
            dma((NJ, NZ)), dma((NJ, 2, 4)),
            dma((NJ,)), dma((NJ,)),
            dma((4,)), dma((4,)),
        ],
        compiler_params=pltpu.CompilerParams(
            collective_id=0, has_side_effects=True, vmem_limit_bytes=60 * 1024 * 1024
        ),
        cost_estimate=pl.CostEstimate(flops=2_400_000_000, bytes_accessed=8_000_000, transcendentals=4_000_000),
    )(query, key, value, out_weight, table)


def solution(mesh):
    places = mesh.shape["seq"] * mesh.shape["blk"]
    call = jax.shard_map(
        shards,
        mesh=mesh,
        in_specs=(
            P("branch", ("seq", "blk"), None),
            P("branch", ("seq", "blk"), None),
            P("branch", ("seq", "blk"), None),
            P("blk", None),
            P(),
        ),
        out_specs=P(("seq", "blk"), "branch"),
        check_vma=False,
    )

    def run(query, key, value, out_weight):
        return call(query, key, value, out_weight, jnp.asarray(tables(places)))

    return run
```

```python
import functools

import jax
import jax.numpy as jnp
import numpy as np
from jax import lax
from jax.experimental import pallas as pl
from jax.experimental.pallas import tpu as pltpu
from jax.sharding import PartitionSpec as P

HD = 128
GRIDW = 256
GUIDANCE = 4.0
F32 = jnp.float32
BF16 = jnp.bfloat16
MESH = pl.DeviceIdType.MESH

NJ = 3
NZ = 8
NY = 4
ROWS = 36
MAIN = 32
REM = ROWS - MAIN
TOK = NZ * ROWS
QS = 4 * TOK
KS = NY * TOK
PART = (0, 48, 80, 112)
SCALE = float(HD**-0.5 / np.log(2.0))


def tables(places):
    time_dim = HD // 8
    side_dim = (HD - time_dim) // 2
    index = np.arange(side_dim // 2).astype(np.float32)
    freq = np.power(np.float32(10000.0), -2.0 * index / side_dim).astype(np.float32)
    at = np.arange(places * ROWS)
    row = (at // GRIDW).astype(np.float32)[:, None] * freq[None, :]
    col = (at % GRIDW).astype(np.float32)[:, None] * freq[None, :]
    still = np.zeros((places * ROWS, time_dim // 2), np.float32)
    angle = np.repeat(np.concatenate([still, row, col], axis=1), 2, axis=1).astype(np.float64)
    sign = np.where(np.arange(HD) % 2 == 0, -1.0, 1.0)
    both = np.stack([np.cos(angle), np.sin(angle) * sign]).astype(np.float32)
    out = np.zeros((places, 2, 40, HD), np.float32)
    out[:, :, :ROWS] = both.reshape(2, places, ROWS, HD).transpose(1, 0, 2, 3)
    return out


def turn(x, cos, sin):
    even = lax.broadcasted_iota(jnp.int32, x.shape, 1) % 2 == 0
    swapped = jnp.where(even, pltpu.roll(x, HD - 1, 1), pltpu.roll(x, 1, 1))
    return x * cos + swapped * sin


def pick(shape, source):
    row = lax.broadcasted_iota(jnp.int32, shape, 0)
    col = lax.broadcasted_iota(jnp.int32, shape, 1)
    return jnp.where(col == source(row), 1.0, 0.0).astype(BF16)


def outward(i):
    return jnp.where(i % 2 == 1, 4 - (i + 1) // 2, 4 + i // 2)


def dot(a, b):
    return jnp.dot(a, b, preferred_element_type=F32)


def kernel(
    q_hbm, k_hbm, v_hbm, w_ref, tab_ref, o_ref,
    q_ref, k_ref, v_ref, tab, rtab, send_a, recv_a, qall, kv, vt, obuf, pst, mo, mst, wt, cbuf,
    recv_c, sib_c, gbuf, acc, dsend, drecv, dsend4, drecv4, wv,
    in_sem, w_sem, a_send, a_recv, q_send, q_recv, y_send, y_recv,
    m_send, m_recv, n_send, n_recv, c_send, c_recv, s_send, s_recv, d_send, d_recv,
):
    c = lax.axis_index("branch")
    s = lax.axis_index("seq")
    xl = lax.axis_index("blk")
    xh = s // 32
    y = (s // 8) % 4
    z = s % 8
    place = s * 2 + xl
    slot = xl * 2 + c

    def far(zz, blk):
        return (xh, (c * 4 + y) * 8 + zz, blk)

    def ring(step):
        return (c, (xh * 4 + (y + step) % 4) * 8 + z, xl)

    def near(step):
        device = ((c + step) % 2, s, (xl + step // 2) % 2)
        return device, device[2] * 2 + device[0]

    loads = [
        pltpu.make_async_copy(src, dst, in_sem.at[i])
        for i, (src, dst) in enumerate(
            ((tab_ref.at[place], tab), (k_hbm.at[0], k_ref), (q_hbm.at[0], q_ref), (v_hbm.at[0], v_ref))
        )
    ]
    for load in loads:
        load.start()

    barrier = pltpu.get_barrier_semaphore()

    @pl.loop(0, NZ)
    def _(zz):
        @pl.when(jnp.logical_not((xh == c) & (zz == z)))
        def _():
            pl.semaphore_signal(barrier, inc=1, device_id=far(zz, xl), device_id_type=MESH)

    for step in range(1, 4):
        pl.semaphore_signal(barrier, inc=1, device_id=ring(step), device_id_type=MESH)
        pl.semaphore_signal(barrier, inc=1, device_id=near(step)[0], device_id_type=MESH)

    w_copies = []
    for j in range(NJ):
        for t in range(4):
            w_copies.append(
                pltpu.make_async_copy(
                    w_ref.at[pl.ds((t * NJ + j) * HD, HD), pl.ds(pl.multiple_of(c * 1536, 1536), 1536)],
                    wv.at[j, pl.ds(t * HD, HD)],
                    w_sem.at[j, t],
                )
            )

    def weights(j):
        for t in range(4):
            w_copies[j * 4 + t].start()

    def own(zz):
        return (xh == c) & (zz == z)

    def a_copy(j, p, zz):
        rows = pl.ds(PART[p], PART[p + 1] - PART[p])
        return pltpu.make_async_remote_copy(
            src_ref=send_a.at[j, zz, rows], dst_ref=recv_a.at[j, z, rows],
            send_sem=a_send.at[j, p, zz], recv_sem=a_recv.at[j, p, z],
            device_id=far(zz, xl), device_id_type=MESH,
        )

    def a_local(j, p):
        rows = pl.ds(PART[p], PART[p + 1] - PART[p])
        return pltpu.make_async_copy(send_a.at[j, z, rows], recv_a.at[j, z, rows], a_recv.at[j, p, z])

    def a_arrival(j, p, zz):
        rows = pl.ds(PART[p], PART[p + 1] - PART[p])
        return pltpu.make_async_remote_copy(
            src_ref=send_a.at[j, zz, rows], dst_ref=recv_a.at[j, zz, rows],
            send_sem=a_send.at[j, p, zz], recv_sem=a_recv.at[j, p, zz],
            device_id=far(zz, xl), device_id_type=MESH,
        )

    for load in loads:
        load.wait()
    rtab[0, 0:4] = tab[0, 32:36] * SCALE
    rtab[0, 4:8] = tab[0, 32:36]
    rtab[1, 0:4] = tab[1, 32:36] * SCALE
    rtab[1, 4:8] = tab[1, 32:36]

    def prepare(j):
        @pl.loop(0, NZ)
        def _(zz):
            cols = pl.ds(pl.multiple_of((zz * NJ + j) * HD, HD), HD)
            cos, sin = tab[0, 0:MAIN], tab[1, 0:MAIN]
            q = turn(q_ref[0:MAIN, cols].astype(F32), cos * SCALE, sin * SCALE)
            k = turn(k_ref[0:MAIN, cols].astype(F32), cos, sin)
            send_a[j, zz, 0:32] = k.astype(BF16)
            send_a[j, zz, 48:80] = v_ref[0:MAIN, cols]
            send_a[j, zz, 80:112] = q.astype(BF16)
            qk = jnp.concatenate(
                [q_ref[MAIN:ROWS, cols].astype(F32), k_ref[MAIN:ROWS, cols].astype(F32)], axis=0
            )
            v4 = v_ref[MAIN:ROWS, cols].astype(F32)
            rest = jnp.concatenate([turn(qk, rtab[0], rtab[1]), v4, jnp.zeros_like(v4)], axis=0)
            send_a[j, zz, 32:48] = rest.astype(BF16)

    def depart(j, p):
        @pl.loop(0, NZ)
        def _(i):
            zz = (z + outward(i)) % NZ

            @pl.when(own(zz))
            def _():
                a_local(j, p).start()

            @pl.when(jnp.logical_not(own(zz)))
            def _():
                a_copy(j, p, zz).start()

    def y_copy(j, p, way):
        return pltpu.make_async_remote_copy(
            src_ref=kv.at[j, 0, p], dst_ref=kv.at[j, 1 + way, p],
            send_sem=y_send.at[j, p, way], recv_sem=y_recv.at[j, p, way],
            device_id=ring((1, 3, 2)[way]), device_id_type=MESH,
        )

    def q_copy(j, step):
        return pltpu.make_async_remote_copy(
            src_ref=qall.at[j, slot], dst_ref=qall.at[j, slot],
            send_sem=q_send.at[j, step - 1], recv_sem=q_recv.at[j, step - 1],
            device_id=near(step)[0], device_id_type=MESH,
        )

    def gather(j, p):
        for zz in range(NZ):
            a_arrival(j, p, zz).wait_recv()
        if p == 0:
            for zz in range(NZ):
                kv[j, 0, 0, zz * 32 : zz * 32 + 32] = recv_a[j, zz, 0:32]
            rest = recv_a[j, :, 32:48, :].reshape(NZ * 16, HD)
            order = pick((96, 128), lambda r: (r % 32) // 4 * 16 + r // 32 * 4 + r % 4)
            rest = dot(order, rest).astype(BF16)
            kv[j, 0, 0, 256:288] = rest[32:64]
            kv[j, 0, 1, 256:288] = rest[64:96]
            qall[j, slot, 256:288] = rest[0:32]
        elif p == 1:
            for zz in range(NZ):
                kv[j, 0, 1, zz * 32 : zz * 32 + 32] = recv_a[j, zz, 48:80]
        else:
            for zz in range(NZ):
                qall[j, slot, zz * 32 : zz * 32 + 32] = recv_a[j, zz, 80:112]
        if p < 2:
            for way in (2, 0, 1):
                y_copy(j, p, way).start()
        else:
            for step in (3, 2, 1):
                q_copy(j, step).start()

    def pieces(j, step):
        return ((128, 160), (0, 128)) if j == NJ - 1 and step > 1 else ((0, TOK),)

    def m_copy(j, step, piece):
        device, other = near(step)
        first, rows = pieces(j, step)[piece]
        return pltpu.make_async_remote_copy(
            src_ref=obuf.at[j, pl.ds(pl.multiple_of(other * TOK + first, 32), rows)],
            dst_ref=mo.at[j, slot, pl.ds(first, rows)],
            send_sem=m_send.at[j, step - 1, piece], recv_sem=m_recv.at[j, step - 1, piece],
            device_id=device, device_id_type=MESH,
        )

    def m_arrival(j, step, piece):
        device, other = near(step)
        rows = pl.ds(*pieces(j, step)[piece])
        return pltpu.make_async_remote_copy(
            src_ref=mo.at[j, slot, rows], dst_ref=mo.at[j, other, rows],
            send_sem=m_send.at[j, step - 1, piece], recv_sem=m_recv.at[j, step - 1, piece],
            device_id=device, device_id_type=MESH,
        )

    def n_copy(j, step):
        device, other = near(step)
        return pltpu.make_async_remote_copy(
            src_ref=pst.at[j, other], dst_ref=mst.at[j, slot],
            send_sem=n_send.at[j, step - 1], recv_sem=n_recv.at[j, step - 1],
            device_id=device, device_id_type=MESH,
        )

    def n_arrival(j, step):
        device, other = near(step)
        return pltpu.make_async_remote_copy(
            src_ref=mst.at[j, slot], dst_ref=mst.at[j, other],
            send_sem=n_send.at[j, step - 1], recv_sem=n_recv.at[j, step - 1],
            device_id=device, device_id_type=MESH,
        )

    def attend_rows(j, first, count):
        queries = qall[j, pl.ds(first, count)].reshape(count * TOK, HD)
        keys = kv[j, :, 0].reshape(KS, HD)
        scores = lax.dot_general(keys, queries, (((1,), (1,)), ((), ())), preferred_element_type=F32)
        top = jnp.max(scores, axis=0, keepdims=True)
        expo = jnp.exp2(scores - top)
        total = jnp.sum(expo, axis=0, keepdims=True)
        mixed = dot(vt[...], expo.astype(BF16)) / total
        obuf[j, pl.ds(pl.multiple_of(first * TOK, 32), count * TOK)] = mixed.T.astype(BF16)
        for i in range(count):
            for r in range(3):
                lanes = slice((2 * i + r) * HD, min((2 * i + r + 1) * HD, count * TOK))
                wide = slice(0, lanes.stop - lanes.start)
                pst[j, first + i, r : r + 1, wide] = top[:, lanes]
                pst[j, first + i, 3 + r : 4 + r, wide] = total[:, lanes]

    def attend(j):
        for step in range(1, 4):
            q_copy(j, step).wait_recv()
        for p in range(2):
            for way in range(3):
                y_copy(j, p, way).wait_recv()
        for t in range(NY):
            vt[:, t * TOK : (t + 1) * TOK] = kv[j, t, 1].astype(F32).T.astype(BF16)
        pst[j] = jnp.ones((4, 8, HD), F32)
        last = j == NJ - 1
        if last:
            attend_rows(j, (1 - xl) * 2, 2)
        else:
            attend_rows(j, 0, 4)
        for step in (3, 2):
            n_copy(j, step).start()
            m_copy(j, step, 0).start()
        if last:
            attend_rows(j, xl * 2, 2)
        n_copy(j, 1).start()
        m_copy(j, 1, 0).start()
        if last:
            for step in (3, 2):
                m_copy(j, step, 1).start()
        mo[j, slot] = obuf[j, pl.ds(pl.multiple_of(slot * TOK, 32), TOK), :]
        mst[j, slot] = pst[j, slot]

    def c_copy(j, zz):
        return pltpu.make_async_remote_copy(
            src_ref=cbuf.at[j, zz], dst_ref=recv_c.at[j, xl, z % 4],
            send_sem=c_send.at[j, zz], recv_sem=c_recv.at[j, xl, z % 4],
            device_id=far(zz, z // 4), device_id_type=MESH,
        )

    def c_own(zz):
        return (xh == c) & (zz == z) & (z // 4 == xl)

    def shares(j):
        for step in range(1, 4):
            n_arrival(j, step).wait_recv()
        tops = [mst[j, i, 0:3, :] for i in range(4)]
        top = jnp.maximum(jnp.maximum(tops[0], tops[1]), jnp.maximum(tops[2], tops[3]))
        parts = [mst[j, i, 3:6, :] * jnp.exp2(tops[i] - top) for i in range(4)]
        total = (parts[0] + parts[1]) + (parts[2] + parts[3])
        parts = [p / total for p in parts]
        for r in range(3):
            rows = jnp.concatenate([p[r : r + 1] for p in parts] + [jnp.zeros((124, HD), F32)], axis=0)
            wt[r * HD : (r + 1) * HD] = rows.T

    def merge_rows(j, first, rows):
        at = c if j == NJ - 1 else slot
        share = wt[pl.ds(pl.multiple_of(at * 32 + first, 32), rows), :]
        mixed = share[:, 0:1] * mo[j, 0, first : first + rows].astype(F32)
        for i in range(1, 4):
            mixed += share[:, i : i + 1] * mo[j, i, first : first + rows].astype(F32)
        mixed = mixed.astype(BF16)
        for n in range(min(rows, 256 - first) // MAIN):
            cbuf[j, first // MAIN + n, 0:32] = mixed[n * MAIN : (n + 1) * MAIN]
        if first + rows == TOK:
            order = pick((128, 32), lambda r: jnp.where(r % 16 < 4, r // 16 * 4 + r % 16, -1))
            rest = dot(order, mixed[256 - first : TOK - first]).astype(BF16)
            for zz in range(NZ):
                cbuf[j, zz, 32:48] = rest[zz * 16 : zz * 16 + 16]

    def c_depart(j, zz):
        @pl.when(c_own(zz))
        def _():
            pltpu.make_async_copy(cbuf.at[j, z], recv_c.at[j, xl, z % 4], c_recv.at[j, xl, z % 4]).start()

        @pl.when(jnp.logical_not(c_own(zz)))
        def _():
            c_copy(j, zz).start()

    def merge(j):
        for step in range(1, 4):
            m_arrival(j, step, 0).wait_recv()
        shares(j)
        if j < NJ - 1:
            merge_rows(j, 0, TOK)
            pl.loop(0, NZ)(lambda i: c_depart(j, (z + outward(i)) % NZ))
        else:
            merge_rows(j, 128, 160)
            pl.loop(0, 4)(lambda i: c_depart(j, 4 + (z + i) % 4))
            for step in (3, 2):
                m_arrival(j, step, 1).wait_recv()
            merge_rows(j, 0, 128)
            pl.loop(0, 4)(lambda i: c_depart(j, (z + i) % 4))

    sibling = (1 - c, s, xl)

    def s_copy(j):
        return pltpu.make_async_remote_copy(
            src_ref=recv_c.at[j], dst_ref=sib_c.at[j],
            send_sem=s_send.at[j], recv_sem=s_recv.at[j],
            device_id=sibling, device_id_type=MESH,
        )

    def share_out(j):
        for blk in range(2):
            for t in range(4):
                pltpu.make_async_remote_copy(
                    src_ref=cbuf.at[j, 0], dst_ref=recv_c.at[j, blk, t],
                    send_sem=c_send.at[j, 0], recv_sem=c_recv.at[j, blk, t],
                    device_id=sibling, device_id_type=MESH,
                ).wait_recv()
        s_copy(j).start()

    mine = jnp.where(c == 0, GUIDANCE, 1.0 - GUIDANCE)
    theirs = 1.0 - mine

    def d_copy(n):
        src, dst = (dsend.at[n], drecv.at[n]) if n < 3 else (dsend4, drecv4)
        return pltpu.make_async_remote_copy(
            src_ref=src, dst_ref=dst,
            send_sem=d_send.at[n], recv_sem=d_recv.at[n],
            device_id=(c, s, 1 - xl), device_id_type=MESH,
        )

    def project(j):
        s_copy(j).wait_recv()
        for blk in range(2):
            for t in range(4):
                g = mine * recv_c[j, blk, t].astype(F32) + theirs * sib_c[j, blk, t].astype(F32)
                gbuf[blk * 48 : blk * 48 + 48, t * HD : (t + 1) * HD] = g.astype(BF16)
        for t in range(4):
            w_copies[j * 4 + t].wait()
        rest = []
        for n in range(3):
            part = dot(gbuf[...], wv[j, :, n * 512 : (n + 1) * 512])
            if j > 0:
                part += acc[n]
            acc[n] = part
            if j == NJ - 1:
                other = pl.multiple_of((1 - xl) * 48, 16)
                dsend[n] = acc[n, pl.ds(other, MAIN), :].astype(BF16)
                d_copy(n).start()
                rest.append(acc[n, pl.ds(other + MAIN, 8), :][0:REM])
        if j == NJ - 1:
            dsend4[...] = jnp.concatenate(rest + [jnp.zeros_like(rest[0])], axis=0).astype(BF16)
            d_copy(3).start()

    prepare(0)
    pl.semaphore_wait(barrier, jnp.where(xh == c, 13, 14))
    depart(0, 0)
    depart(0, 1)
    depart(0, 2)
    prepare(1)
    depart(1, 0)
    depart(1, 1)
    depart(1, 2)
    prepare(2)
    depart(2, 0)
    depart(2, 1)
    depart(2, 2)
    gather(0, 0)
    gather(0, 1)
    gather(0, 2)
    gather(1, 0)
    gather(1, 1)
    gather(1, 2)
    attend(0)
    gather(2, 0)
    gather(2, 1)
    gather(2, 2)
    attend(1)
    weights(0)
    merge(0)
    attend(2)
    weights(1)
    weights(2)
    merge(1)
    share_out(0)
    project(0)
    merge(2)
    share_out(1)
    project(1)
    share_out(2)
    project(2)

    mine_at = pl.multiple_of(xl * 48, 16)
    for n in range(3):
        d_copy(n).wait_recv()
        full = acc[n, pl.ds(mine_at, MAIN), :] + drecv[n].astype(F32)
        o_ref[0:MAIN, n * 512 : (n + 1) * 512] = full.astype(BF16)
    d_copy(3).wait_recv()
    rest = drecv4[...].astype(F32)
    for n in range(3):
        full = acc[n, pl.ds(mine_at + MAIN, 8), :][0:REM] + rest[n * REM : (n + 1) * REM]
        o_ref[MAIN:ROWS, n * 512 : (n + 1) * 512] = full.astype(BF16)

    for j in range(NJ):
        @pl.loop(0, NZ)
        def _(zz):
            @pl.when(jnp.logical_not(own(zz)))
            def _():
                for p in range(3):
                    a_copy(j, p, zz).wait_send()

            @pl.when(jnp.logical_not(c_own(zz)))
            def _():
                c_copy(j, zz).wait_send()

        for step in range(1, 4):
            q_copy(j, step).wait_send()
            n_copy(j, step).wait_send()
            for piece in range(len(pieces(j, step))):
                m_copy(j, step, piece).wait_send()
        for p in range(2):
            for way in range(3):
                y_copy(j, p, way).wait_send()
        s_copy(j).wait_send()
    for n in range(4):
        d_copy(n).wait_send()


def shards(query, key, value, out_weight, table):
    hbm = pl.BlockSpec(memory_space=pl.ANY)
    dma = pltpu.SemaphoreType.DMA
    return pl.pallas_call(
        kernel,
        out_shape=pltpu.VMEM((ROWS, 1536), BF16),
        in_specs=[hbm] * 5,
        out_specs=pl.BlockSpec(memory_space=pltpu.VMEM),
        scratch_shapes=[
            pltpu.VMEM((ROWS, 3072), BF16),
            pltpu.VMEM((ROWS, 3072), BF16),
            pltpu.VMEM((ROWS, 3072), BF16),
            pltpu.VMEM((2, 40, HD), F32),
            pltpu.VMEM((2, 8, HD), F32),
            pltpu.VMEM((NJ, NZ, 112, HD), BF16),
            pltpu.VMEM((NJ, NZ, 112, HD), BF16),
            pltpu.VMEM((NJ, 4, TOK, HD), BF16),
            pltpu.VMEM((NJ, NY, 2, TOK, HD), BF16),
            pltpu.VMEM((HD, KS), BF16),
            pltpu.VMEM((NJ, QS, HD), BF16),
            pltpu.VMEM((NJ, 4, 8, HD), F32),
            pltpu.VMEM((NJ, 4, TOK, HD), BF16),
            pltpu.VMEM((NJ, 4, 8, HD), F32),
            pltpu.VMEM((3 * HD, HD), F32),
            pltpu.VMEM((NJ, NZ, 48, HD), BF16),
            pltpu.VMEM((NJ, 2, 4, 48, HD), BF16),
            pltpu.VMEM((NJ, 2, 4, 48, HD), BF16),
            pltpu.VMEM((96, 512), BF16),
            pltpu.VMEM((3, 96, 512), F32),
            pltpu.VMEM((3, 32, 512), BF16),
            pltpu.VMEM((3, 32, 512), BF16),
            pltpu.VMEM((16, 512), BF16),
            pltpu.VMEM((16, 512), BF16),
            pltpu.VMEM((NJ, 512, 1536), BF16),
            dma((4,)), dma((NJ, 4)),
            dma((NJ, 3, NZ)), dma((NJ, 3, NZ)),
            dma((NJ, 3)), dma((NJ, 3)),
            dma((NJ, 2, 3)), dma((NJ, 2, 3)),
            dma((NJ, 3, 2)), dma((NJ, 3, 2)),
            dma((NJ, 3)), dma((NJ, 3)),
            dma((NJ, NZ)), dma((NJ, 2, 4)),
            dma((NJ,)), dma((NJ,)),
            dma((4,)), dma((4,)),
        ],
        compiler_params=pltpu.CompilerParams(
            collective_id=0, has_side_effects=True, vmem_limit_bytes=60 * 1024 * 1024
        ),
        cost_estimate=pl.CostEstimate(flops=2_400_000_000, bytes_accessed=8_000_000, transcendentals=4_000_000),
    )(query, key, value, out_weight, table)


def solution(mesh):
    places = mesh.shape["seq"] * mesh.shape["blk"]
    call = jax.shard_map(
        shards,
        mesh=mesh,
        in_specs=(
            P("branch", ("seq", "blk"), None),
            P("branch", ("seq", "blk"), None),
            P("branch", ("seq", "blk"), None),
            P("blk", None),
            P(),
        ),
        out_specs=P(("seq", "blk"), "branch"),
        check_vma=False,
    )

    def run(query, key, value, out_weight):
        return call(query, key, value, out_weight, jnp.asarray(tables(places)))

    return run
```
